512 devices in a mesh: dp: 64 (over x, z, core), tp: 8 (over y).
Axes of the slice: x: 4, y: 8, z: 8, core: 2. Of those that a mesh axis runs over, the one named last changes fastest.
Arguments:
- normed_layer_input: bfloat16 [18432, 7168], P('dp', 'tp'), may hold values from -6 to 6
- queries: bfloat16 [16384, 7168], P('dp', 'tp'), may hold values from -100 to 100
- saved_key_rows: bfloat16 [18432, 1024], P('dp', 'tp'), may hold values from -4.5 to 4.5
- saved_value_rows: bfloat16 [18432, 1024], P('dp', 'tp'), may hold values from -6 to 6
- attention_output_gradient: bfloat16 [16384, 7168], P('dp', 'tp'), may hold values from -6 to 6
- finisher_token_mask: int32 [16384], P('dp'), may hold values 0 or 1
- response_length: int32 [64], P('dp'), may hold values from 128 to 256
- value_weight_matrix: bfloat16 [1024, 7168], P('tp'), may hold values from -0.0625 to 0.0625
- adapter_down_factor: bfloat16 [7168, 64], P('tp'), may hold values from -0.0625 to 0.0625
- adapter_up_factor: bfloat16 [64, 1024], P(None, 'tp'), may hold values from -0.75 to 0.75
Outputs:
- layer_input_gradient: bfloat16 [18432, 7168], P('dp', 'tp')
- query_grad: bfloat16 [16384, 7168], P('dp', 'tp')
- key_grad: bfloat16 [18432, 1024], P('dp', 'tp')
- down_factor_gradient: float32 [7168, 64], P('tp')
- up_factor_gradient: float32 [64, 1024], P(None, 'tp')
The draws below stay inside these ranges and needn't reach their ends.
All inputs are finite; a program needn't handle non-finite values. No bound on the sum of `finisher_token_mask` on one device may be relied on, other than what follows from the above.
Results may differ from the reference program's by a relative error of at most 0.02.
Values may be sent and summed in bfloat16 or wider, within the bound.
A program may use at most 64 MiB of HBM per device.

```python
import math
import jax
import jax.numpy as jnp
from jax import lax

MODEL_WIDTH = 7168
QH = 56
KVH = 8
HD = 128
ADAPTER_RANK = 64
RESP = 256
CTX = 288
GROUPS = 64
TOKENS = 18432
RTOKENS = 16384
QD = 7168
KEY_VALUE_WIDTH = 1024
N_TP = 8


def base_keys(key):
    return jnp.clip(jax.random.normal(key, (TOKENS, KEY_VALUE_WIDTH), jnp.float32), -4.5, 4.5)


def draw_saved_key_rows(key, part):
    raw = base_keys(key)
    return raw.astype(jnp.bfloat16)


def draw_queries(key, part):
    key = jax.random.fold_in(key, 5)
    drawn = jnp.clip(jax.random.normal(key, (RTOKENS, QD), jnp.float32), -4.5, 4.5)
    return drawn.astype(jnp.bfloat16)


def touch_ends(values, own_key, low, top_value):
    longest = values.shape.index(max(values.shape))
    spots = []
    for shift in (0, 1):
        where = [jax.random.randint(jax.random.fold_in(own_key, axis), (), 0, length) for axis, length in enumerate(values.shape)]
        where[longest] = (where[longest] + shift) % values.shape[longest]
        spots.append(tuple(where))
    return values.at[spots[0]].set(low).at[spots[1]].set(top_value)


def levels(rng, dims, split, least, largest):
    loudness, own = 1.0, jax.random.fold_in(rng, 6)
    for axis_at, blocks in split:
        steps = jnp.exp(jax.random.uniform(jax.random.fold_in(own, axis_at), (blocks,), jnp.float32, least / len(split), largest / len(split)))
        loudness = loudness * jnp.repeat(steps, dims[axis_at] // blocks).reshape([-1 if axis == axis_at else 1 for axis in range(len(dims))])
    return loudness


def bell_draw(stream_key, dims, deviation, limit, split=(), held_as=jnp.bfloat16):
    level = levels(stream_key, dims, split, -0.22, 0.18) if split else 1.0
    values = jax.random.normal(stream_key, dims, jnp.float32) * deviation * level
    return jnp.minimum(jnp.maximum(values, -limit), limit).astype(held_as)


def setup_inputs(seed: int = 0) -> dict:
    streams_of = jax.random.split(jax.random.key(seed), 11)
    return {
        "normed_layer_input": bell_draw(streams_of[0], (TOKENS, MODEL_WIDTH), 1.0, 6.0, ((0, 64), (1, 8))),
        "queries": draw_queries(jax.random.fold_in(streams_of[10], 71), 0),
        "saved_key_rows": draw_saved_key_rows(jax.random.fold_in(streams_of[10], 71), 0),
        "saved_value_rows": bell_draw(streams_of[3], (TOKENS, KEY_VALUE_WIDTH), 1.0, 6.0, ((0, 64), (1, 8))),
        "attention_output_gradient": bell_draw(streams_of[4], (RTOKENS, QD), 1.0, 6.0, ((0, 64), (1, 8))),
        "finisher_token_mask": touch_ends((jax.random.randint(streams_of[5], (RTOKENS,), 0, 4) < 3).astype(jnp.int32), jax.random.fold_in(streams_of[5], 1), 0, 1),
        "response_length": touch_ends(jax.random.randint(streams_of[6], (GROUPS,), RESP // 2, RESP + 1), jax.random.fold_in(streams_of[6], 1), RESP // 2, RESP).astype(jnp.int32),
        "value_weight_matrix": bell_draw(streams_of[7], (KEY_VALUE_WIDTH, MODEL_WIDTH), MODEL_WIDTH ** -0.5, 0.0625, ((0, 8),)),
        "adapter_down_factor": bell_draw(streams_of[8], (MODEL_WIDTH, ADAPTER_RANK), MODEL_WIDTH ** -0.5, 0.0625, ((0, 8),)),
        "adapter_up_factor": bell_draw(streams_of[9], (ADAPTER_RANK, KEY_VALUE_WIDTH), ADAPTER_RANK ** -0.5, 0.75, ((1, 8),)),
    }


adapter_scale = 2.0

def group_grads(queries, saved_key_rows, saved_value_rows, attention_output_gradient, mask_row, length):
    replies = queries.shape[0]
    context = saved_key_rows.shape[0]
    prompt = context - replies
    group_size = QH // KVH
    factor = 1.0 / math.sqrt(HD)
    q_heads = queries.astype(jnp.float32).reshape(replies, KVH, group_size, HD)
    k_heads = saved_key_rows.astype(jnp.float32).reshape(context, KVH, HD)
    v_heads = saved_value_rows.astype(jnp.float32).reshape(context, KVH, HD)
    row_ids = jnp.arange(replies, dtype=jnp.int32)
    keep = jnp.where(row_ids < length, mask_row, 0)
    grad_rows = (attention_output_gradient.astype(jnp.float32) * keep[:, None].astype(jnp.float32)).reshape(replies, KVH, group_size, HD)
    col_ids = jnp.arange(context, dtype=jnp.int32)[None, :]
    visible = (col_ids <= prompt + row_ids[:, None]) & ((col_ids < prompt) | (col_ids - prompt < length))
    scores = jnp.einsum('rxgd,cxd->xgrc', q_heads, k_heads) * factor
    scores = jnp.where(visible[None, None], scores, -1e+30)
    top = lax.optimization_barrier(jnp.max(scores, axis=-1, keepdims=True))
    expo = jnp.exp(scores - top)
    probs = expo / lax.optimization_barrier(jnp.sum(expo, axis=-1, keepdims=True))
    probs_low = lax.optimization_barrier(probs.astype(jnp.bfloat16)).astype(jnp.float32)
    dprobs = jnp.einsum('rxgd,cxd->xgrc', grad_rows, v_heads)
    dscores = probs * (dprobs - lax.optimization_barrier(jnp.sum(probs * dprobs, axis=-1, keepdims=True))) * factor
    dscores_low = lax.optimization_barrier(dscores.astype(jnp.bfloat16)).astype(jnp.float32)
    query_grad = jnp.einsum('xgrc,cxd->rxgd', dscores_low, k_heads).reshape(replies, -1).astype(jnp.bfloat16)
    key_grad = jnp.einsum('xgrc,rxgd->cxd', dscores_low, q_heads).reshape(context, -1).astype(jnp.bfloat16)
    value_rows_gradient = jnp.einsum('xgrc,rxgd->cxd', probs_low, grad_rows).reshape(context, -1).astype(jnp.bfloat16)
    return (query_grad, key_grad, value_rows_gradient)

def reference(normed_layer_input, queries, saved_key_rows, saved_value_rows, attention_output_gradient, finisher_token_mask, response_length, value_weight_matrix, adapter_down_factor, adapter_up_factor):
    groups = response_length.shape[0]
    packed = (queries.reshape(groups, RESP, -1), saved_key_rows.reshape(groups, CTX, -1), saved_value_rows.reshape(groups, CTX, -1), attention_output_gradient.reshape(groups, RESP, -1), finisher_token_mask.reshape(groups, RESP), response_length)
    query_grad, key_grad, value_rows_gradient = lax.map(lambda item: group_grads(*item), packed)
    query_grad = query_grad.reshape(groups * RESP, -1)
    key_grad = key_grad.reshape(groups * CTX, -1)
    value_rows_gradient = value_rows_gradient.reshape(groups * CTX, -1)
    block = KVH * HD // N_TP
    frozen_value_output = jnp.zeros((groups * CTX, MODEL_WIDTH), jnp.float32)
    for block_idx in range(N_TP):
        start = block_idx * block
        term = jnp.dot(value_rows_gradient[:, start:start + block], value_weight_matrix[start:start + block], preferred_element_type=jnp.float32)
        frozen_value_output = frozen_value_output + lax.optimization_barrier(term.astype(jnp.bfloat16)).astype(jnp.float32)
    down_activation_rows = jnp.dot(normed_layer_input, adapter_down_factor, preferred_element_type=jnp.float32).astype(jnp.bfloat16)
    up_backward_rows = jnp.dot(value_rows_gradient, adapter_up_factor.T, preferred_element_type=jnp.float32).astype(jnp.bfloat16)
    layer_input_gradient = (frozen_value_output + adapter_scale * jnp.dot(up_backward_rows, adapter_down_factor.T, preferred_element_type=jnp.float32)).astype(jnp.bfloat16)
    down_factor_gradient = adapter_scale * lax.dot_general(normed_layer_input, up_backward_rows, (((0,), (0,)), ((), ())), preferred_element_type=jnp.float32)
    up_factor_gradient = adapter_scale * lax.dot_general(down_activation_rows, value_rows_gradient, (((0,), (0,)), ((), ())), preferred_element_type=jnp.float32)
    return (layer_input_gradient, query_grad, key_grad, down_factor_gradient, up_factor_gradient)
```

```python
import math

import jax
import jax.numpy as jnp
from jax import lax
from jax.experimental import pallas as pl
from jax.experimental.pallas import tpu as pltpu
from jax.sharding import PartitionSpec as P

MESH = pl.DeviceIdType.MESH
BF16 = jnp.bfloat16
F32 = jnp.float32

QH = 56
KVH = 8
HD = 128
HEADS = QH // KVH
RESP = 256
CTX = 288
PROMPT = CTX - RESP
RANK = 64
FEATS = 896
FACTOR = 1.0 / math.sqrt(HD)
LOG2E = math.log2(math.e)
adapter_scale = 2.0

NX, NZ, NC, NY = 4, 8, 2, 8
ROWS = 16

RB = 128
SEEN = (PROMPT + RB, CTX)

NT = (((1,), (1,)), ((), ()))


def dot(a, b):
    return jnp.dot(a, b, preferred_element_type=F32)


def dot_nt(a, b):
    return lax.dot_general(a, b, NT, preferred_element_type=F32)


def rows_of_heads(ref, b):
    return jnp.concatenate(
        [ref[b * RB : (b + 1) * RB, h * HD : (h + 1) * HD] for h in range(HEADS)], axis=0
    )


def kernel(
    x_hbm, q_hbm, k_hbm, v_hbm, g_hbm, mask_ref, length_ref, w_hbm, at_hbm, b_hbm,
    lig_ref, qg_ref, kg_ref, dfg_ref, ufg_ref,
    x_ref, q_ref, k_ref, v_ref, g_ref, at_ref,
    wfull, bfull, vgfull,
    p0, p1, pb0, pb1,
    dpart, dpieces, dfull,
    rs_src, rs_dst, bc_buf, ag_buf,
    load_sem, w1_send, w1_recv, wz_send, wz_recv, wx_send, wx_recv, wc_send, wc_recv,
    b_send, b_recv, d1_send, d1_recv, d2_send, d2_recv, vg_send, vg_recv,
    rs_send, rs_recv, bc_send, bc_recv, ag_send, ag_recv,
):
    dp = lax.axis_index("dp")
    y = lax.axis_index("tp")
    x = dp // (NZ * NC)
    z = (dp // NC) % NZ
    c = dp % NC

    def at(px, pz, pc, py):
        return {"dp": (px * NZ + pz) * NC + pc, "tp": py}

    y_to = [(y + k) % NY for k in range(1, NY)]
    y_from = [(y + NY - k) % NY for k in range(1, NY)]
    z_to = [(z + k) % NZ for k in range(1, NZ)]
    z_from = [(z + NZ - k) % NZ for k in range(1, NZ)]
    x_to = [(x + k) % NX for k in range(1, NX)]
    x_from = [(x + NX - k) % NX for k in range(1, NX)]
    xc_steps = [(i, j) for i in range(NX) for j in range(NC) if i or j]
    xc_to = [((x + i) % NX, (c + j) % NC) for i, j in xc_steps]
    xc_from = [((x + NX - i) % NX, (c + NC - j) % NC) for i, j in xc_steps]
    y_dev = [at(x, z, c, j) for j in y_to]
    z_dev = [at(x, j, c, y) for j in z_to]
    x_dev = [at(j, z, c, y) for j in x_to]
    xc_dev = [at(i, z, j, y) for i, j in xc_to]
    sibling = at(x, z, 1 - c, y)

    def remote(src, dst, send, recv, device):
        return pltpu.make_async_remote_copy(
            src_ref=src, dst_ref=dst, send_sem=send, recv_sem=recv, device_id=device, device_id_type=MESH
        )

    pending = []

    def fan_out(src, dst, send, recv, devices):
        for k, device in enumerate(devices):
            copy = remote(src(k), dst, send.at[k], recv.at[k], device)
            copy.start()
            pending.append(copy)

    def landed(dst, send, recv, devices):
        for k, device in enumerate(devices):
            remote(dst(k), dst(k), send.at[k], recv.at[k], device).wait_recv()

    barrier = pltpu.get_barrier_semaphore()
    everyone = y_dev + z_dev + xc_dev
    for device in everyone:
        pl.semaphore_signal(barrier, inc=1, device_id=device, device_id_type=MESH)

    w_y = 4 * c + x
    w_rows = pl.ds(pl.multiple_of(z * ROWS, ROWS), ROWS)

    def w_cols(j):
        return pl.ds(pl.multiple_of(j * FEATS, 128), FEATS)

    loads = [
        pltpu.make_async_copy(src, dst, load_sem.at[i])
        for i, (src, dst) in enumerate(
            [
                (x_hbm, x_ref),
                (at_hbm, at_ref),
                (k_hbm, k_ref),
                (q_hbm, q_ref),
                (g_hbm, g_ref),
                (v_hbm, v_ref),
                (b_hbm, bfull.at[y]),
            ]
        )
    ]
    for load in loads:
        load.start()
    load_x, load_a, load_k, load_q, load_g, load_v, load_b = loads
    w_own = pltpu.make_async_copy(w_hbm.at[w_rows, w_cols(y)], wfull.at[w_y, z], load_sem.at[7])

    @pl.when(y == w_y)
    def _():
        w_own.start()

    load_x.wait()
    load_a.wait()
    dpart[...] = dot_nt(at_ref[...], x_ref[...]).reshape(dpart.shape)
    load_b.wait()

    pl.semaphore_wait(barrier, len(everyone))

    @pl.when(y == w_y)
    def _():
        for k in range(NY - 1):
            remote(
                w_hbm.at[w_rows, w_cols(y_to[k])], wfull.at[w_y, z], w1_send.at[k], w1_recv, y_dev[k]
            ).start()

    fan_out(lambda k: dpart.at[y_to[k]], dpieces.at[y], d1_send, d1_recv, y_dev)
    fan_out(lambda k: bfull.at[y], bfull.at[y], b_send, b_recv, y_dev)

    load_k.wait()
    load_q.wait()
    limit = PROMPT - 1 + length_ref[0]
    probs = (p0, p1)
    probs_low = (pb0, pb1)

    def weigh(b, h):
        seen = SEEN[b]
        q = q_ref[b * RB : (b + 1) * RB, h * HD : (h + 1) * HD]
        scores = dot_nt(k_ref[:seen, :], q) * (FACTOR * LOG2E)
        col = lax.broadcasted_iota(jnp.int32, (seen, RB), 0)
        row = lax.broadcasted_iota(jnp.int32, (1, RB), 1) + b * RB
        last = jnp.minimum(row + PROMPT, limit)
        scores = jnp.where(col <= last, scores, -1e30)
        top = jnp.max(scores, axis=0, keepdims=True)
        expo = jnp.exp2(scores - top)
        keep = jnp.where(row + PROMPT <= limit, mask_ref[:, b * RB : (b + 1) * RB], 0).astype(F32)
        p = expo * (keep / jnp.sum(expo, axis=0, keepdims=True))
        probs[b][:, h * HD : (h + 1) * HD] = p
        probs_low[b][:, h * HD : (h + 1) * HD] = p.astype(BF16)

    for h in range(HEADS):
        for b in range(2):
            weigh(b, h)
        if h == 1:
            @pl.when(y == w_y)
            def _():
                w_own.wait()

            @pl.when(y != w_y)
            def _():
                remote(wfull.at[w_y, z], wfull.at[w_y, z], w1_send.at[0], w1_recv, y_dev[0]).wait_recv()

            fan_out(lambda k: wfull.at[w_y, z], wfull.at[w_y, z], wz_send, wz_recv, z_dev)
        if h == 3:
            landed(lambda k: dpieces.at[y_from[k]], d1_send, d1_recv, y_dev)
            total = dpart[y]
            for k in range(NY - 1):
                total = total + dpieces[y_from[k]]
            dfull[y] = total
            fan_out(lambda k: dfull.at[y], dfull.at[y], d2_send, d2_recv, y_dev)
        if h == 5:
            landed(lambda k: wfull.at[w_y, z_from[k]], wz_send, wz_recv, z_dev)
            fan_out(lambda k: wfull.at[w_y], wfull.at[w_y], wx_send, wx_recv, x_dev)

    load_g.wait()
    early = dot(pb0[...], rows_of_heads(g_ref, 0))
    late = dot(pb1[...], rows_of_heads(g_ref, 1))
    vgfull[y, : SEEN[0], :] = (early + late[: SEEN[0]]).astype(BF16)
    vgfull[y, SEEN[0] :, :] = late[SEEN[0] :].astype(BF16)
    fan_out(lambda k: vgfull.at[y], vgfull.at[y], vg_send, vg_recv, y_dev)

    load_v.wait()
    for h in range(HEADS):
        for b in range(2):
            seen = SEEN[b]
            lanes = slice(h * HD, (h + 1) * HD)
            p = probs[b][:, lanes]
            t = p * dot_nt(v_ref[:seen, :], g_ref[b * RB : (b + 1) * RB, lanes])
            probs_low[b][:, lanes] = ((t - p * jnp.sum(t, axis=0, keepdims=True)) * FACTOR).astype(BF16)

    early = dot(pb0[...], rows_of_heads(q_ref, 0))
    late = dot(pb1[...], rows_of_heads(q_ref, 1))
    kg_ref[: SEEN[0], :] = (early + late[: SEEN[0]]).astype(BF16)
    kg_ref[SEEN[0] :, :] = late[SEEN[0] :].astype(BF16)
    keys_t = k_ref[...].astype(F32).T.astype(BF16)
    for b in range(2):
        qg_t = dot(keys_t[:, : SEEN[b]], probs_low[b][...])
        for h in range(HEADS):
            lanes = slice(h * HD, (h + 1) * HD)
            qg_ref[b * RB : (b + 1) * RB, lanes] = qg_t[:, lanes].T.astype(BF16)

    landed(lambda k: dfull.at[y_from[k]], d2_send, d2_recv, y_dev)
    rs_src[NZ - 1] = dot(dfull[...].reshape(RANK, CTX).astype(BF16), vgfull[y]).astype(BF16)

    landed(lambda k: wfull.at[4 * c + x_from[k]], wx_send, wx_recv, x_dev)
    half = pl.ds(4 * c, 4)
    other = pl.ds(4 * (1 - c), 4)
    to_sibling = remote(wfull.at[half], wfull.at[half], wc_send.at[0], wc_recv.at[0], sibling)
    to_sibling.start()

    landed(lambda k: bfull.at[y_from[k]], b_send, b_recv, y_dev)
    landed(lambda k: vgfull.at[y_from[k]], vg_send, vg_recv, y_dev)
    values = jnp.concatenate([vgfull[j] for j in range(NY)], axis=1)
    ups = jnp.concatenate([bfull[j] for j in range(NY)], axis=1)
    up_t = dot_nt(ups, values).astype(BF16)
    dfg_t = dot(up_t, x_ref[...])
    for j in range(NZ - 1):
        rs_src[j] = dfg_t[:, j * 128 : (j + 1) * 128].astype(BF16)

    fan_out(lambda k: rs_src.at[z_to[k]], rs_dst.at[z], rs_send, rs_recv, z_dev)

    up = dot_nt(values, ups).astype(BF16)
    remote(wfull.at[other], wfull.at[other], wc_send.at[0], wc_recv.at[0], sibling).wait_recv()

    def input_gradient(low, high):
        w = wfull[:, :, :, low:high].reshape(NY * HD, high - low)
        frozen = dot(values, w)
        adapter = dot(up, at_ref[:, low:high])
        lig_ref[:, low:high] = (frozen + adapter_scale * adapter).astype(BF16)

    input_gradient(0, 256)

    landed(lambda k: rs_dst.at[z_from[k]], rs_send, rs_recv, z_dev)
    total = rs_src[z].astype(F32)
    for k in range(NZ - 1):
        total = total + rs_dst[z_from[k]].astype(F32)
    bc_buf[x * NC + c] = total.astype(BF16)
    fan_out(lambda k: bc_buf.at[x * NC + c], bc_buf.at[x * NC + c], bc_send, bc_recv, xc_dev)

    input_gradient(256, 512)

    landed(lambda k: bc_buf.at[xc_from[k][0] * NC + xc_from[k][1]], bc_send, bc_recv, xc_dev)
    total = bc_buf[0].astype(F32)
    for j in range(1, NX * NC):
        total = total + bc_buf[j].astype(F32)
    ag_buf[z] = total.astype(BF16)
    fan_out(lambda k: ag_buf.at[z], ag_buf.at[z], ag_send, ag_recv, z_dev)

    input_gradient(512, 896)

    landed(lambda k: ag_buf.at[z_from[k]], ag_send, ag_recv, z_dev)
    for j in range(NZ - 1):
        dfg_ref[:, j * 128 : (j + 1) * 128] = adapter_scale * ag_buf[j].astype(F32)
    ufg_ref[...] = adapter_scale * ag_buf[NZ - 1].astype(F32)

    for copy in pending:
        copy.wait_send()
    to_sibling.wait_send()

    @pl.when(y == w_y)
    def _():
        for k in range(NY - 1):
            remote(
                w_hbm.at[w_rows, w_cols(y_to[k])], wfull.at[w_y, z], w1_send.at[k], w1_recv, y_dev[k]
            ).wait_send()


def per_device(
    normed_layer_input,
    queries,
    saved_key_rows,
    saved_value_rows,
    attention_output_gradient,
    finisher_token_mask,
    response_length,
    value_weight_matrix,
    adapter_down_factor,
    adapter_up_factor,
):
    hbm = pl.BlockSpec(memory_space=pl.ANY)
    vmem = pl.BlockSpec(memory_space=pltpu.VMEM)
    smem = pl.BlockSpec(memory_space=pltpu.SMEM)
    dma = pltpu.SemaphoreType.DMA
    lig, qg, kg, dfg_t, ufg = pl.pallas_call(
        kernel,
        out_shape=(
            jax.ShapeDtypeStruct((CTX, FEATS), BF16),
            jax.ShapeDtypeStruct((RESP, FEATS), BF16),
            jax.ShapeDtypeStruct((CTX, HD), BF16),
            jax.ShapeDtypeStruct((RANK, FEATS), F32),
            jax.ShapeDtypeStruct((RANK, HD), F32),
        ),
        in_specs=[hbm, hbm, hbm, hbm, hbm, vmem, smem, hbm, hbm, hbm],
        out_specs=(vmem,) * 5,
        scratch_shapes=[
            pltpu.VMEM((CTX, FEATS), BF16),
            pltpu.VMEM((RESP, FEATS), BF16),
            pltpu.VMEM((CTX, HD), BF16),
            pltpu.VMEM((CTX, HD), BF16),
            pltpu.VMEM((RESP, FEATS), BF16),
            pltpu.VMEM((RANK, FEATS), BF16),
            pltpu.VMEM((NY, NZ, ROWS, FEATS), BF16),
            pltpu.VMEM((NY, RANK, HD), BF16),
            pltpu.VMEM((NY, CTX, HD), BF16),
            pltpu.VMEM((SEEN[0], FEATS), F32),
            pltpu.VMEM((SEEN[1], FEATS), F32),
            pltpu.VMEM((SEEN[0], FEATS), BF16),
            pltpu.VMEM((SEEN[1], FEATS), BF16),
            pltpu.VMEM((NY, RANK // NY, CTX), F32),
            pltpu.VMEM((NY, RANK // NY, CTX), F32),
            pltpu.VMEM((NY, RANK // NY, CTX), F32),
            pltpu.VMEM((NZ, RANK, HD), BF16),
            pltpu.VMEM((NZ, RANK, HD), BF16),
            pltpu.VMEM((NX * NC, RANK, HD), BF16),
            pltpu.VMEM((NZ, RANK, HD), BF16),
            dma((8,)),
            dma((NY - 1,)),
            dma,
            dma((NZ - 1,)),
            dma((NZ - 1,)),
            dma((NX - 1,)),
            dma((NX - 1,)),
            dma((1,)),
            dma((1,)),
            dma((NY - 1,)),
            dma((NY - 1,)),
            dma((NY - 1,)),
            dma((NY - 1,)),
            dma((NY - 1,)),
            dma((NY - 1,)),
            dma((NY - 1,)),
            dma((NY - 1,)),
            dma((NZ - 1,)),
            dma((NZ - 1,)),
            dma((NX * NC - 1,)),
            dma((NX * NC - 1,)),
            dma((NZ - 1,)),
            dma((NZ - 1,)),
        ],
        compiler_params=pltpu.CompilerParams(
            collective_id=0, has_side_effects=True, vmem_limit_bytes=40 * 1024 * 1024
        ),
    )(
        normed_layer_input,
        queries,
        saved_key_rows,
        saved_value_rows,
        attention_output_gradient,
        finisher_token_mask.reshape(1, RESP),
        response_length,
        value_weight_matrix,
        adapter_down_factor.T,
        adapter_up_factor,
    )
    return (lig, qg, kg, dfg_t.T, ufg)


def solution(mesh):
    in_specs = (
        P("dp", "tp"),
        P("dp", "tp"),
        P("dp", "tp"),
        P("dp", "tp"),
        P("dp", "tp"),
        P("dp"),
        P("dp"),
        P("tp", None),
        P("tp", None),
        P(None, "tp"),
    )
    out_specs = (P("dp", "tp"), P("dp", "tp"), P("dp", "tp"), P("tp", None), P(None, "tp"))
    return jax.shard_map(
        per_device, mesh=mesh, in_specs=in_specs, out_specs=out_specs, check_vma=False
    )
```

```python
import math

import jax
import jax.numpy as jnp
from jax import lax
from jax.experimental import pallas as pl
from jax.experimental.pallas import tpu as pltpu
from jax.sharding import PartitionSpec as P

MESH = pl.DeviceIdType.MESH
BF16 = jnp.bfloat16
F32 = jnp.float32

QH = 56
KVH = 8
HD = 128
HEADS = QH // KVH
RESP = 256
CTX = 288
PROMPT = CTX - RESP
RANK = 64
FEATS = 896
FACTOR = 1.0 / math.sqrt(HD)
LOG2E = math.log2(math.e)
adapter_scale = 2.0

NX, NZ, NC, NY = 4, 8, 2, 8
ROWS = 16

RB = 128
SEEN = (PROMPT + RB, CTX)

VMEM_LIMIT = 60 * 1024 * 1024

NT = (((1,), (1,)), ((), ()))


def dot(a, b):
    return jnp.dot(a, b, preferred_element_type=F32)


def dot_nt(a, b):
    return lax.dot_general(a, b, NT, preferred_element_type=F32)


def rows_of_heads(ref, b):
    return jnp.concatenate(
        [ref[b * RB : (b + 1) * RB, h * HD : (h + 1) * HD] for h in range(HEADS)], axis=0
    )


def kernel(
    x_hbm, q_hbm, k_hbm, v_hbm, g_hbm, mask_hbm, length_hbm, w_hbm, at_hbm, b_hbm,
    lig_hbm, qg_hbm, kg_hbm, dfg_hbm, ufg_hbm,
    x_ref, q_ref, k_ref, v_ref, g_ref, at_ref, mask_ref, length_ref,
    wfull, bfull, vgfull,
    p0, p1, pb0, pb1,
    dpart, dpieces, dfull,
    rs_src, rs_dst, bc_buf, ag_buf,
    lig_ref, qg_ref, kg_ref, dfg_ref, ufg_ref,
    load_sem, store_sem, w1_send, w1_recv, wz_send, wz_recv, wx_send, wx_recv, wc_send, wc_recv,
    b_send, b_recv, d1_send, d1_recv, d2_send, d2_recv, vg_send, vg_recv,
    rs_send, rs_recv, bc_send, bc_recv, ag_send, ag_recv,
):
    dp = lax.axis_index("dp")
    y = lax.axis_index("tp")
    x = dp // (NZ * NC)
    z = (dp // NC) % NZ
    c = dp % NC

    def at(px, pz, pc, py):
        return {"dp": (px * NZ + pz) * NC + pc, "tp": py}

    y_to = [(y + k) % NY for k in range(1, NY)]
    y_from = [(y + NY - k) % NY for k in range(1, NY)]
    z_to = [(z + k) % NZ for k in range(1, NZ)]
    z_from = [(z + NZ - k) % NZ for k in range(1, NZ)]
    x_to = [(x + k) % NX for k in range(1, NX)]
    x_from = [(x + NX - k) % NX for k in range(1, NX)]
    xc_steps = [(i, j) for i in range(NX) for j in range(NC) if i or j]
    xc_to = [((x + i) % NX, (c + j) % NC) for i, j in xc_steps]
    xc_from = [((x + NX - i) % NX, (c + NC - j) % NC) for i, j in xc_steps]
    y_dev = [at(x, z, c, j) for j in y_to]
    z_dev = [at(x, j, c, y) for j in z_to]
    x_dev = [at(j, z, c, y) for j in x_to]
    xc_dev = [at(i, z, j, y) for i, j in xc_to]
    sibling = at(x, z, 1 - c, y)

    def remote(src, dst, send, recv, device):
        return pltpu.make_async_remote_copy(
            src_ref=src, dst_ref=dst, send_sem=send, recv_sem=recv, device_id=device, device_id_type=MESH
        )

    pending = []
    stores = [
        pltpu.make_async_copy(src, dst, store_sem.at[i])
        for i, (src, dst) in enumerate(
            [(lig_ref, lig_hbm), (qg_ref, qg_hbm), (kg_ref, kg_hbm), (dfg_ref, dfg_hbm), (ufg_ref, ufg_hbm)]
        )
    ]

    def fan_out(src, dst, send, recv, devices):
        for k, device in enumerate(devices):
            copy = remote(src(k), dst, send.at[k], recv.at[k], device)
            copy.start()
            pending.append(copy)

    def landed(dst, send, recv, devices):
        for k, device in enumerate(devices):
            remote(dst(k), dst(k), send.at[k], recv.at[k], device).wait_recv()

    barrier = pltpu.get_barrier_semaphore()
    everyone = y_dev + z_dev + xc_dev
    for device in everyone:
        pl.semaphore_signal(barrier, inc=1, device_id=device, device_id_type=MESH)

    w_y = 4 * c + x
    w_rows = pl.ds(pl.multiple_of(z * ROWS, ROWS), ROWS)

    def w_cols(j):
        return pl.ds(pl.multiple_of(j * FEATS, 128), FEATS)

    loads = [
        pltpu.make_async_copy(src, dst, load_sem.at[i])
        for i, (src, dst) in enumerate(
            [
                (x_hbm, x_ref),
                (at_hbm, at_ref),
                (k_hbm, k_ref),
                (q_hbm, q_ref),
                (g_hbm, g_ref),
                (v_hbm, v_ref),
                (b_hbm, bfull.at[y]),
                (mask_hbm, mask_ref),
                (length_hbm, length_ref),
            ]
        )
    ]
    for load in loads:
        load.start()
    load_x, load_a, load_k, load_q, load_g, load_v, load_b, load_mask, load_length = loads
    w_own = pltpu.make_async_copy(w_hbm.at[w_rows, w_cols(y)], wfull.at[w_y, z], load_sem.at[9])

    @pl.when(y == w_y)
    def _():
        w_own.start()

    load_x.wait()
    load_a.wait()
    dpart[...] = dot_nt(at_ref[...], x_ref[...]).reshape(dpart.shape)
    load_b.wait()

    pl.semaphore_wait(barrier, len(everyone))

    @pl.when(y == w_y)
    def _():
        for k in range(NY - 1):
            remote(
                w_hbm.at[w_rows, w_cols(y_to[k])], wfull.at[w_y, z], w1_send.at[k], w1_recv, y_dev[k]
            ).start()

    fan_out(lambda k: dpart.at[y_to[k]], dpieces.at[y], d1_send, d1_recv, y_dev)
    fan_out(lambda k: bfull.at[y], bfull.at[y], b_send, b_recv, y_dev)

    load_k.wait()
    load_q.wait()
    load_mask.wait()
    load_length.wait()
    limit = PROMPT - 1 + length_ref[0]
    probs = (p0, p1)
    probs_low = (pb0, pb1)

    def weigh(b, h):
        seen = SEEN[b]
        q = q_ref[b * RB : (b + 1) * RB, h * HD : (h + 1) * HD]
        scores = dot_nt(k_ref[:seen, :], q) * (FACTOR * LOG2E)
        col = lax.broadcasted_iota(jnp.int32, (seen, RB), 0)
        row = lax.broadcasted_iota(jnp.int32, (1, RB), 1) + b * RB
        last = jnp.minimum(row + PROMPT, limit)
        scores = jnp.where(col <= last, scores, -1e30)
        top = jnp.max(scores, axis=0, keepdims=True)
        expo = jnp.exp2(scores - top)
        keep = jnp.where(row + PROMPT <= limit, mask_ref[:, b * RB : (b + 1) * RB], 0).astype(F32)
        p = expo * (keep / jnp.sum(expo, axis=0, keepdims=True))
        probs[b][:, h * HD : (h + 1) * HD] = p
        probs_low[b][:, h * HD : (h + 1) * HD] = p.astype(BF16)

    for h in range(HEADS):
        for b in range(2):
            weigh(b, h)
        if h == 1:
            @pl.when(y == w_y)
            def _():
                w_own.wait()

            @pl.when(y != w_y)
            def _():
                remote(wfull.at[w_y, z], wfull.at[w_y, z], w1_send.at[0], w1_recv, y_dev[0]).wait_recv()

            fan_out(lambda k: wfull.at[w_y, z], wfull.at[w_y, z], wz_send, wz_recv, z_dev)
        if h == 3:
            landed(lambda k: dpieces.at[y_from[k]], d1_send, d1_recv, y_dev)
            total = dpart[y]
            for k in range(NY - 1):
                total = total + dpieces[y_from[k]]
            dfull[y] = total
            fan_out(lambda k: dfull.at[y], dfull.at[y], d2_send, d2_recv, y_dev)
        if h == 5:
            landed(lambda k: wfull.at[w_y, z_from[k]], wz_send, wz_recv, z_dev)
            fan_out(lambda k: wfull.at[w_y], wfull.at[w_y], wx_send, wx_recv, x_dev)

    load_g.wait()
    early = dot(pb0[...], rows_of_heads(g_ref, 0))
    late = dot(pb1[...], rows_of_heads(g_ref, 1))
    vgfull[y, : SEEN[0], :] = (early + late[: SEEN[0]]).astype(BF16)
    vgfull[y, SEEN[0] :, :] = late[SEEN[0] :].astype(BF16)
    fan_out(lambda k: vgfull.at[y], vgfull.at[y], vg_send, vg_recv, y_dev)

    load_v.wait()
    for h in range(HEADS):
        for b in range(2):
            seen = SEEN[b]
            lanes = slice(h * HD, (h + 1) * HD)
            p = probs[b][:, lanes]
            t = p * dot_nt(v_ref[:seen, :], g_ref[b * RB : (b + 1) * RB, lanes])
            probs_low[b][:, lanes] = ((t - p * jnp.sum(t, axis=0, keepdims=True)) * FACTOR).astype(BF16)

    early = dot(pb0[...], rows_of_heads(q_ref, 0))
    late = dot(pb1[...], rows_of_heads(q_ref, 1))
    kg_ref[: SEEN[0], :] = (early + late[: SEEN[0]]).astype(BF16)
    kg_ref[SEEN[0] :, :] = late[SEEN[0] :].astype(BF16)
    keys_t = k_ref[...].astype(F32).T.astype(BF16)
    for b in range(2):
        qg_t = dot(keys_t[:, : SEEN[b]], probs_low[b][...])
        for h in range(HEADS):
            lanes = slice(h * HD, (h + 1) * HD)
            qg_ref[b * RB : (b + 1) * RB, lanes] = qg_t[:, lanes].T.astype(BF16)

    stores[1].start()
    stores[2].start()

    landed(lambda k: dfull.at[y_from[k]], d2_send, d2_recv, y_dev)
    rs_src[NZ - 1] = dot(dfull[...].reshape(RANK, CTX).astype(BF16), vgfull[y]).astype(BF16)

    landed(lambda k: wfull.at[4 * c + x_from[k]], wx_send, wx_recv, x_dev)
    half = pl.ds(4 * c, 4)
    other = pl.ds(4 * (1 - c), 4)
    to_sibling = remote(wfull.at[half], wfull.at[half], wc_send.at[0], wc_recv.at[0], sibling)
    to_sibling.start()

    landed(lambda k: bfull.at[y_from[k]], b_send, b_recv, y_dev)
    landed(lambda k: vgfull.at[y_from[k]], vg_send, vg_recv, y_dev)
    values = jnp.concatenate([vgfull[j] for j in range(NY)], axis=1)
    ups = jnp.concatenate([bfull[j] for j in range(NY)], axis=1)
    up_t = dot_nt(ups, values).astype(BF16)
    dfg_t = dot(up_t, x_ref[...])
    for j in range(NZ - 1):
        rs_src[j] = dfg_t[:, j * 128 : (j + 1) * 128].astype(BF16)

    fan_out(lambda k: rs_src.at[z_to[k]], rs_dst.at[z], rs_send, rs_recv, z_dev)

    up = dot_nt(values, ups).astype(BF16)
    remote(wfull.at[other], wfull.at[other], wc_send.at[0], wc_recv.at[0], sibling).wait_recv()

    def input_gradient(low, high):
        w = wfull[:, :, :, low:high].reshape(NY * HD, high - low)
        frozen = dot(values, w)
        adapter = dot(up, at_ref[:, low:high])
        lig_ref[:, low:high] = (frozen + adapter_scale * adapter).astype(BF16)

    input_gradient(0, 256)

    landed(lambda k: rs_dst.at[z_from[k]], rs_send, rs_recv, z_dev)
    total = rs_src[z].astype(F32)
    for k in range(NZ - 1):
        total = total + rs_dst[z_from[k]].astype(F32)
    bc_buf[x * NC + c] = total.astype(BF16)
    fan_out(lambda k: bc_buf.at[x * NC + c], bc_buf.at[x * NC + c], bc_send, bc_recv, xc_dev)

    input_gradient(256, 512)

    landed(lambda k: bc_buf.at[xc_from[k][0] * NC + xc_from[k][1]], bc_send, bc_recv, xc_dev)
    total = bc_buf[0].astype(F32)
    for j in range(1, NX * NC):
        total = total + bc_buf[j].astype(F32)
    ag_buf[z] = total.astype(BF16)
    fan_out(lambda k: ag_buf.at[z], ag_buf.at[z], ag_send, ag_recv, z_dev)

    input_gradient(512, 896)
    stores[0].start()

    landed(lambda k: ag_buf.at[z_from[k]], ag_send, ag_recv, z_dev)
    for j in range(NZ - 1):
        dfg_ref[:, j * 128 : (j + 1) * 128] = adapter_scale * ag_buf[j].astype(F32)
    ufg_ref[...] = adapter_scale * ag_buf[NZ - 1].astype(F32)
    stores[3].start()
    stores[4].start()

    for copy in pending:
        copy.wait_send()
    to_sibling.wait_send()
    for store in stores:
        store.wait()

    @pl.when(y == w_y)
    def _():
        for k in range(NY - 1):
            remote(
                w_hbm.at[w_rows, w_cols(y_to[k])], wfull.at[w_y, z], w1_send.at[k], w1_recv, y_dev[k]
            ).wait_send()


def hand_on(*refs):
    sems = refs[10]
    copies = [pltpu.make_async_copy(refs[i], refs[5 + i], sems.at[i]) for i in range(5)]
    for copy in copies:
        copy.start()
    for copy in copies:
        copy.wait()


def per_device(
    normed_layer_input,
    queries,
    saved_key_rows,
    saved_value_rows,
    attention_output_gradient,
    finisher_token_mask,
    response_length,
    value_weight_matrix,
    adapter_down_factor,
    adapter_up_factor,
):
    hbm = pl.BlockSpec(memory_space=pltpu.HBM)
    dma = pltpu.SemaphoreType.DMA
    outs = pl.pallas_call(
        kernel,
        out_shape=(
            jax.ShapeDtypeStruct((CTX, FEATS), BF16),
            jax.ShapeDtypeStruct((RESP, FEATS), BF16),
            jax.ShapeDtypeStruct((CTX, HD), BF16),
            jax.ShapeDtypeStruct((RANK, FEATS), F32),
            jax.ShapeDtypeStruct((RANK, HD), F32),
        ),
        in_specs=[hbm] * 10,
        out_specs=(hbm,) * 5,
        scratch_shapes=[
            pltpu.VMEM((CTX, FEATS), BF16),
            pltpu.VMEM((RESP, FEATS), BF16),
            pltpu.VMEM((CTX, HD), BF16),
            pltpu.VMEM((CTX, HD), BF16),
            pltpu.VMEM((RESP, FEATS), BF16),
            pltpu.VMEM((RANK, FEATS), BF16),
            pltpu.VMEM((1, RESP), jnp.int32),
            pltpu.SMEM((1,), jnp.int32),
            pltpu.VMEM((NY, NZ, ROWS, FEATS), BF16),
            pltpu.VMEM((NY, RANK, HD), BF16),
            pltpu.VMEM((NY, CTX, HD), BF16),
            pltpu.VMEM((SEEN[0], FEATS), F32),
            pltpu.VMEM((SEEN[1], FEATS), F32),
            pltpu.VMEM((SEEN[0], FEATS), BF16),
            pltpu.VMEM((SEEN[1], FEATS), BF16),
            pltpu.VMEM((NY, RANK // NY, CTX), F32),
            pltpu.VMEM((NY, RANK // NY, CTX), F32),
            pltpu.VMEM((NY, RANK // NY, CTX), F32),
            pltpu.VMEM((NZ, RANK, HD), BF16),
            pltpu.VMEM((NZ, RANK, HD), BF16),
            pltpu.VMEM((NX * NC, RANK, HD), BF16),
            pltpu.VMEM((NZ, RANK, HD), BF16),
            pltpu.VMEM((CTX, FEATS), BF16),
            pltpu.VMEM((RESP, FEATS), BF16),
            pltpu.VMEM((CTX, HD), BF16),
            pltpu.VMEM((RANK, FEATS), F32),
            pltpu.VMEM((RANK, HD), F32),
            dma((10,)),
            dma((5,)),
            dma((NY - 1,)),
            dma,
            dma((NZ - 1,)),
            dma((NZ - 1,)),
            dma((NX - 1,)),
            dma((NX - 1,)),
            dma((1,)),
            dma((1,)),
            dma((NY - 1,)),
            dma((NY - 1,)),
            dma((NY - 1,)),
            dma((NY - 1,)),
            dma((NY - 1,)),
            dma((NY - 1,)),
            dma((NY - 1,)),
            dma((NY - 1,)),
            dma((NZ - 1,)),
            dma((NZ - 1,)),
            dma((NX * NC - 1,)),
            dma((NX * NC - 1,)),
            dma((NZ - 1,)),
            dma((NZ - 1,)),
        ],
        compiler_params=pltpu.CompilerParams(
            collective_id=0, has_side_effects=True, vmem_limit_bytes=VMEM_LIMIT
        ),
    )(
        normed_layer_input,
        queries,
        saved_key_rows,
        saved_value_rows,
        attention_output_gradient,
        finisher_token_mask.reshape(1, RESP),
        response_length,
        value_weight_matrix,
        adapter_down_factor.T,
        adapter_up_factor,
    )
    lig, qg, kg, dfg_t, ufg = pl.pallas_call(
        hand_on,
        out_shape=[jax.ShapeDtypeStruct(out.shape, out.dtype) for out in outs],
        in_specs=[pl.BlockSpec(memory_space=pl.ANY)] * 5,
        out_specs=[hbm] * 5,
        scratch_shapes=[dma((5,))],
        compiler_params=pltpu.CompilerParams(vmem_limit_bytes=VMEM_LIMIT),
    )(*outs)
    return (lig, qg, kg, dfg_t.T, ufg)


def solution(mesh):
    in_specs = (
        P("dp", "tp"),
        P("dp", "tp"),
        P("dp", "tp"),
        P("dp", "tp"),
        P("dp", "tp"),
        P("dp"),
        P("dp"),
        P("tp", None),
        P("tp", None),
        P(None, "tp"),
    )
    out_specs = (P("dp", "tp"), P("dp", "tp"), P("dp", "tp"), P("tp", None), P(None, "tp"))
    return jax.shard_map(
        per_device, mesh=mesh, in_specs=in_specs, out_specs=out_specs, check_vma=False
    )
```

```python
import math

import jax
import jax.numpy as jnp
from jax import lax
from jax.experimental import pallas as pl
from jax.experimental.pallas import tpu as pltpu
from jax.sharding import PartitionSpec as P

MESH = pl.DeviceIdType.MESH
BF16 = jnp.bfloat16
F32 = jnp.float32

QH = 56
KVH = 8
HD = 128
HEADS = QH // KVH
RESP = 256
CTX = 288
PROMPT = CTX - RESP
RANK = 64
FEATS = 896
FACTOR = 1.0 / math.sqrt(HD)
LOG2E = math.log2(math.e)
adapter_scale = 2.0

NX, NZ, NC, NY = 4, 8, 2, 8
HALF = CTX // 2
ROWS = 16

FAR_FIRST = (4, 3, 5, 2, 6, 1, 7)

RB = 128
SEEN = (PROMPT + RB, CTX)

VMEM_LIMIT = 60 * 1024 * 1024

NT = (((1,), (1,)), ((), ()))


def dot(a, b):
    return jnp.dot(a, b, preferred_element_type=F32)


def dot_nt(a, b):
    return lax.dot_general(a, b, NT, preferred_element_type=F32)


def rows_of_heads(ref, b):
    return jnp.concatenate(
        [ref[b * RB : (b + 1) * RB, h * HD : (h + 1) * HD] for h in range(HEADS)], axis=0
    )


def kernel(
    x_hbm, q_hbm, k_hbm, v_hbm, g_hbm, mask_hbm, length_hbm, w_hbm, at_hbm, b_hbm,
    lig_hbm, qg_hbm, kg_hbm, sums_hbm,
    x_ref, q_ref, k_ref, v_ref, g_ref, at_ref, mask_ref, length_ref,
    b_ref, wfull, vgfull,
    p0, p1, pb0, pb1,
    downs, ups,
    rs_src, rs_dst, bc_buf, ag_buf,
    lig_ref, qg_ref, kg_ref,
    load_sem, store_sem, w1_send, w1_recv, wz_send, wz_recv, wx_send, wx_recv, wc_send, wc_recv,
    down_send, down_recv, up_send, up_recv, vg_send, vg_recv,
    rs_send, rs_recv, bc_send, bc_recv, ag_send, ag_recv,
):
    dp = lax.axis_index("dp")
    y = lax.axis_index("tp")
    x = dp // (NZ * NC)
    z = (dp // NC) % NZ
    c = dp % NC

    def at(px, pz, pc, py):
        return {"dp": (px * NZ + pz) * NC + pc, "tp": py}

    y_to = [(y + k) % NY for k in FAR_FIRST]
    y_from = [(y + NY - k) % NY for k in FAR_FIRST]
    z_to = [(z + k) % NZ for k in FAR_FIRST]
    z_from = [(z + NZ - k) % NZ for k in FAR_FIRST]
    x_to = [(x + k) % NX for k in (2, 1, 3)]
    x_from = [(x + NX - k) % NX for k in (2, 1, 3)]
    xc_steps = [(i, j) for i in (2, 1, 3, 0) for j in (1, 0) if i or j]
    xc_to = [((x + i) % NX, (c + j) % NC) for i, j in xc_steps]
    xc_from = [((x + NX - i) % NX, (c + NC - j) % NC) for i, j in xc_steps]
    y_dev = [at(x, z, c, j) for j in y_to]
    z_dev = [at(x, j, c, y) for j in z_to]
    x_dev = [at(j, z, c, y) for j in x_to]
    xc_dev = [at(i, z, j, y) for i, j in xc_to]
    sibling = at(x, z, 1 - c, y)

    def remote(src, dst, send, recv, device):
        return pltpu.make_async_remote_copy(
            src_ref=src, dst_ref=dst, send_sem=send, recv_sem=recv, device_id=device, device_id_type=MESH
        )

    pending = []
    stores = [
        pltpu.make_async_copy(src, dst, store_sem.at[i])
        for i, (src, dst) in enumerate(
            [(lig_ref, lig_hbm), (qg_ref, qg_hbm), (kg_ref, kg_hbm), (ag_buf, sums_hbm)]
        )
    ]

    def fan_out(src, dst, send, recv, devices):
        for k, device in enumerate(devices):
            copy = remote(src(k), dst, send.at[k], recv.at[k], device)
            copy.start()
            pending.append(copy)

    def landed(dst, send, recv, devices):
        for k, device in enumerate(devices):
            remote(dst(k), dst(k), send.at[k], recv.at[k], device).wait_recv()

    barrier = pltpu.get_barrier_semaphore()
    everyone = y_dev + z_dev + xc_dev
    for device in everyone:
        pl.semaphore_signal(barrier, inc=1, device_id=device, device_id_type=MESH)

    w_y = 4 * c + x
    w_rows = pl.ds(pl.multiple_of(z * ROWS, ROWS), ROWS)

    def w_cols(j):
        return pl.ds(pl.multiple_of(j * FEATS, 128), FEATS)

    loads = [
        pltpu.make_async_copy(src, dst, load_sem.at[i])
        for i, (src, dst) in enumerate(
            [
                (x_hbm, x_ref),
                (at_hbm, at_ref),
                (k_hbm, k_ref),
                (q_hbm, q_ref),
                (g_hbm, g_ref),
                (v_hbm, v_ref),
                (b_hbm, b_ref),
                (mask_hbm, mask_ref),
                (length_hbm, length_ref),
            ]
        )
    ]
    for load in loads:
        load.start()
    load_x, load_a, load_k, load_q, load_g, load_v, load_b, load_mask, load_length = loads
    w_own = pltpu.make_async_copy(w_hbm.at[w_rows, w_cols(y)], wfull.at[w_y, z], load_sem.at[9])

    @pl.when(y == w_y)
    def _():
        w_own.start()

    def first(factor):
        return jnp.concatenate([factor, jnp.zeros_like(factor)], axis=0)

    def second(factor):
        return jnp.concatenate([jnp.zeros_like(factor), factor], axis=0)

    def rank_rows(rows, factor):
        return dot_nt(rows[:HALF], first(factor)) + dot_nt(rows[HALF:], second(factor))

    def over_tokens(pairs, rows):
        pairs_t = pairs.T.astype(BF16)
        return dot(pairs_t, rows[:HALF])[:RANK] + dot(pairs_t, rows[HALF:])[RANK:]

    def sum_of(parts):
        total = parts[0].astype(F32)
        for j in range(1, parts.shape[0]):
            total = total + parts[j].astype(F32)
        return total

    load_x.wait()
    load_a.wait()
    downs[y] = rank_rows(x_ref, at_ref[...]).astype(BF16)

    pl.semaphore_wait(barrier, len(everyone))

    @pl.when(y == w_y)
    def _():
        for k in range(NY - 1):
            remote(
                w_hbm.at[w_rows, w_cols(y_to[k])], wfull.at[w_y, z], w1_send.at[k], w1_recv, y_dev[k]
            ).start()

    fan_out(lambda k: downs.at[y], downs.at[y], down_send, down_recv, y_dev)

    load_k.wait()
    load_q.wait()
    load_mask.wait()
    load_length.wait()
    limit = PROMPT - 1 + length_ref[0]
    probs = (p0, p1)
    probs_low = (pb0, pb1)

    def weigh(b, h):
        seen = SEEN[b]
        q = q_ref[b * RB : (b + 1) * RB, h * HD : (h + 1) * HD]
        scores = dot_nt(k_ref[:seen, :], q) * (FACTOR * LOG2E)
        col = lax.broadcasted_iota(jnp.int32, (seen, RB), 0)
        row = lax.broadcasted_iota(jnp.int32, (1, RB), 1) + b * RB
        last = jnp.minimum(row + PROMPT, limit)
        scores = jnp.where(col <= last, scores, -1e30)
        top = jnp.max(scores, axis=0, keepdims=True)
        expo = jnp.exp2(scores - top)
        keep = jnp.where(row + PROMPT <= limit, mask_ref[:, b * RB : (b + 1) * RB], 0).astype(F32)
        p = expo * (keep / jnp.sum(expo, axis=0, keepdims=True))
        probs[b][:, h * HD : (h + 1) * HD] = p
        probs_low[b][:, h * HD : (h + 1) * HD] = p.astype(BF16)

    for h in range(HEADS):
        for b in range(2):
            weigh(b, h)

    load_g.wait()
    early = dot(pb0[...], rows_of_heads(g_ref, 0))
    late = dot(pb1[...], rows_of_heads(g_ref, 1))
    vgfull[y, : SEEN[0], :] = (early + late[: SEEN[0]]).astype(BF16)
    vgfull[y, SEEN[0] :, :] = late[SEEN[0] :].astype(BF16)
    load_b.wait()
    own_values = vgfull[y]
    ups[y] = rank_rows(own_values, b_ref[...]).astype(BF16)
    fan_out(lambda k: ups.at[y], ups.at[y], up_send, up_recv, y_dev)
    fan_out(lambda k: vgfull.at[y], vgfull.at[y], vg_send, vg_recv, y_dev)

    @pl.when(y == w_y)
    def _():
        w_own.wait()

    @pl.when(y != w_y)
    def _():
        remote(wfull.at[w_y, z], wfull.at[w_y, z], w1_send.at[0], w1_recv, y_dev[0]).wait_recv()

    fan_out(lambda k: wfull.at[w_y, z], wfull.at[w_y, z], wz_send, wz_recv, z_dev)

    load_v.wait()
    for h in range(HEADS):
        for b in range(2):
            seen = SEEN[b]
            lanes = slice(h * HD, (h + 1) * HD)
            p = probs[b][:, lanes]
            t = p * dot_nt(v_ref[:seen, :], g_ref[b * RB : (b + 1) * RB, lanes])
            probs_low[b][:, lanes] = ((t - p * jnp.sum(t, axis=0, keepdims=True)) * FACTOR).astype(BF16)

    early = dot(pb0[...], rows_of_heads(q_ref, 0))
    late = dot(pb1[...], rows_of_heads(q_ref, 1))
    kg_ref[: SEEN[0], :] = (early + late[: SEEN[0]]).astype(BF16)
    kg_ref[SEEN[0] :, :] = late[SEEN[0] :].astype(BF16)
    keys_t = k_ref[...].astype(F32).T.astype(BF16)
    for b in range(2):
        qg_t = dot(keys_t[:, : SEEN[b]], probs_low[b][...])
        for h in range(HEADS):
            lanes = slice(h * HD, (h + 1) * HD)
            qg_ref[b * RB : (b + 1) * RB, lanes] = qg_t[:, lanes].T.astype(BF16)

    stores[1].start()
    stores[2].start()

    landed(lambda k: downs.at[y_from[k]], down_send, down_recv, y_dev)
    rs_src[NZ - 1] = over_tokens(sum_of(downs), own_values).astype(BF16)
    landed(lambda k: ups.at[y_from[k]], up_send, up_recv, y_dev)
    up = sum_of(ups)
    dfg_t = over_tokens(up, x_ref)
    for j in range(NZ - 1):
        rs_src[j] = dfg_t[:, j * 128 : (j + 1) * 128].astype(BF16)

    fan_out(lambda k: rs_src.at[z_to[k]], rs_dst.at[z], rs_send, rs_recv, z_dev)

    landed(lambda k: wfull.at[w_y, z_from[k]], wz_send, wz_recv, z_dev)
    fan_out(lambda k: wfull.at[w_y], wfull.at[w_y], wx_send, wx_recv, x_dev)

    landed(lambda k: rs_dst.at[z_from[k]], rs_send, rs_recv, z_dev)
    total = rs_src[z].astype(F32)
    for k in range(NZ - 1):
        total = total + rs_dst[z_from[k]].astype(F32)
    bc_buf[x * NC + c] = total.astype(BF16)
    fan_out(lambda k: bc_buf.at[x * NC + c], bc_buf.at[x * NC + c], bc_send, bc_recv, xc_dev)

    landed(lambda k: wfull.at[4 * c + x_from[k]], wx_send, wx_recv, x_dev)
    half = pl.ds(4 * c, 4)
    other = pl.ds(4 * (1 - c), 4)
    to_sibling = remote(wfull.at[half], wfull.at[half], wc_send.at[0], wc_recv.at[0], sibling)
    to_sibling.start()

    landed(lambda k: bc_buf.at[xc_from[k][0] * NC + xc_from[k][1]], bc_send, bc_recv, xc_dev)
    ag_buf[z] = sum_of(bc_buf).astype(BF16)
    fan_out(lambda k: ag_buf.at[z], ag_buf.at[z], ag_send, ag_recv, z_dev)

    landed(lambda k: vgfull.at[y_from[k]], vg_send, vg_recv, y_dev)
    remote(wfull.at[other], wfull.at[other], wc_send.at[0], wc_recv.at[0], sibling).wait_recv()
    values = jnp.concatenate([vgfull[j] for j in range(NY)], axis=1)
    up = up.astype(BF16)
    for low, high in ((0, 256), (256, 512), (512, 768), (768, 896)):
        frozen = dot(values, wfull[:, :, :, low:high].reshape(NY * HD, high - low))
        down = at_ref[:, low:high]
        for rows, factor in ((slice(0, HALF), first(down)), (slice(HALF, CTX), second(down))):
            lig_ref[rows, low:high] = (frozen[rows] + adapter_scale * dot(up, factor)).astype(BF16)
    stores[0].start()

    landed(lambda k: ag_buf.at[z_from[k]], ag_send, ag_recv, z_dev)
    stores[3].start()

    for copy in pending:
        copy.wait_send()
    to_sibling.wait_send()
    for store in stores:
        store.wait()

    @pl.when(y == w_y)
    def _():
        for k in range(NY - 1):
            remote(
                w_hbm.at[w_rows, w_cols(y_to[k])], wfull.at[w_y, z], w1_send.at[k], w1_recv, y_dev[k]
            ).wait_send()


def hand_on(
    lig_hbm, qg_hbm, kg_hbm, sums_hbm,
    lig_out, qg_out, kg_out, dfg_out, ufg_out,
    lig, qg, kg, sums, dfg, ufg, sems,
):
    ins = [
        pltpu.make_async_copy(src, via, sems.at[i])
        for i, (src, via) in enumerate([(sums_hbm, sums), (lig_hbm, lig), (qg_hbm, qg), (kg_hbm, kg)])
    ]
    outs = [
        pltpu.make_async_copy(via, dst, sems.at[4 + i])
        for i, (via, dst) in enumerate([(lig, lig_out), (qg, qg_out), (kg, kg_out), (dfg, dfg_out), (ufg, ufg_out)])
    ]
    for copy in ins:
        copy.start()
    for i in range(3):
        ins[i + 1].wait()
        outs[i].start()
    ins[0].wait()
    for j in range(NZ - 1):
        dfg[:, j * 128 : (j + 1) * 128] = adapter_scale * sums[j].astype(F32)
    outs[3].start()
    ufg[...] = adapter_scale * sums[NZ - 1].astype(F32)
    outs[4].start()
    for copy in outs:
        copy.wait()


def per_device(
    normed_layer_input,
    queries,
    saved_key_rows,
    saved_value_rows,
    attention_output_gradient,
    finisher_token_mask,
    response_length,
    value_weight_matrix,
    adapter_down_factor,
    adapter_up_factor,
):
    hbm = pl.BlockSpec(memory_space=pltpu.HBM)
    dma = pltpu.SemaphoreType.DMA
    outs = pl.pallas_call(
        kernel,
        out_shape=(
            jax.ShapeDtypeStruct((CTX, FEATS), BF16),
            jax.ShapeDtypeStruct((RESP, FEATS), BF16),
            jax.ShapeDtypeStruct((CTX, HD), BF16),
            jax.ShapeDtypeStruct((NZ, RANK, HD), BF16),
        ),
        in_specs=[hbm] * 10,
        out_specs=(hbm,) * 4,
        scratch_shapes=[
            pltpu.VMEM((CTX, FEATS), BF16),
            pltpu.VMEM((RESP, FEATS), BF16),
            pltpu.VMEM((CTX, HD), BF16),
            pltpu.VMEM((CTX, HD), BF16),
            pltpu.VMEM((RESP, FEATS), BF16),
            pltpu.VMEM((RANK, FEATS), BF16),
            pltpu.VMEM((1, RESP), jnp.int32),
            pltpu.SMEM((1,), jnp.int32),
            pltpu.VMEM((RANK, HD), BF16),
            pltpu.VMEM((NY, NZ, ROWS, FEATS), BF16),
            pltpu.VMEM((NY, CTX, HD), BF16),
            pltpu.VMEM((SEEN[0], FEATS), F32),
            pltpu.VMEM((SEEN[1], FEATS), F32),
            pltpu.VMEM((SEEN[0], FEATS), BF16),
            pltpu.VMEM((SEEN[1], FEATS), BF16),
            pltpu.VMEM((NY, HALF, HD), BF16),
            pltpu.VMEM((NY, HALF, HD), BF16),
            pltpu.VMEM((NZ, RANK, HD), BF16),
            pltpu.VMEM((NZ, RANK, HD), BF16),
            pltpu.VMEM((NX * NC, RANK, HD), BF16),
            pltpu.VMEM((NZ, RANK, HD), BF16),
            pltpu.VMEM((CTX, FEATS), BF16),
            pltpu.VMEM((RESP, FEATS), BF16),
            pltpu.VMEM((CTX, HD), BF16),
            dma((10,)),
            dma((4,)),
            dma((NY - 1,)),
            dma,
            dma((NZ - 1,)),
            dma((NZ - 1,)),
            dma((NX - 1,)),
            dma((NX - 1,)),
            dma((1,)),
            dma((1,)),
            dma((NY - 1,)),
            dma((NY - 1,)),
            dma((NY - 1,)),
            dma((NY - 1,)),
            dma((NY - 1,)),
            dma((NY - 1,)),
            dma((NZ - 1,)),
            dma((NZ - 1,)),
            dma((NX * NC - 1,)),
            dma((NX * NC - 1,)),
            dma((NZ - 1,)),
            dma((NZ - 1,)),
        ],
        compiler_params=pltpu.CompilerParams(
            collective_id=0, has_side_effects=True, vmem_limit_bytes=VMEM_LIMIT
        ),
    )(
        normed_layer_input,
        queries,
        saved_key_rows,
        saved_value_rows,
        attention_output_gradient,
        finisher_token_mask.reshape(1, RESP),
        response_length,
        value_weight_matrix,
        adapter_down_factor.T,
        adapter_up_factor,
    )
    lig, qg, kg, dfg_t, ufg = pl.pallas_call(
        hand_on,
        out_shape=(
            jax.ShapeDtypeStruct((CTX, FEATS), BF16),
            jax.ShapeDtypeStruct((RESP, FEATS), BF16),
            jax.ShapeDtypeStruct((CTX, HD), BF16),
            jax.ShapeDtypeStruct((RANK, FEATS), F32),
            jax.ShapeDtypeStruct((RANK, HD), F32),
        ),
        in_specs=[hbm] * 4,
        out_specs=(hbm,) * 5,
        scratch_shapes=[
            pltpu.VMEM((CTX, FEATS), BF16),
            pltpu.VMEM((RESP, FEATS), BF16),
            pltpu.VMEM((CTX, HD), BF16),
            pltpu.VMEM((NZ, RANK, HD), BF16),
            pltpu.VMEM((RANK, FEATS), F32),
            pltpu.VMEM((RANK, HD), F32),
            dma((9,)),
        ],
        compiler_params=pltpu.CompilerParams(vmem_limit_bytes=VMEM_LIMIT),
    )(*outs)
    return (lig, qg, kg, dfg_t.T, ufg)


def solution(mesh):
    in_specs = (
        P("dp", "tp"),
        P("dp", "tp"),
        P("dp", "tp"),
        P("dp", "tp"),
        P("dp", "tp"),
        P("dp"),
        P("dp"),
        P("tp", None),
        P("tp", None),
        P(None, "tp"),
    )
    out_specs = (P("dp", "tp"), P("dp", "tp"), P("dp", "tp"), P("tp", None), P(None, "tp"))
    return jax.shard_map(
        per_device, mesh=mesh, in_specs=in_specs, out_specs=out_specs, check_vma=False
    )
```

```python
import math

import jax
import jax.numpy as jnp
from jax import lax
from jax.experimental import pallas as pl
from jax.experimental.pallas import tpu as pltpu
from jax.sharding import PartitionSpec as P

MESH = pl.DeviceIdType.MESH
BF16 = jnp.bfloat16
F32 = jnp.float32

QH = 56
KVH = 8
HD = 128
HEADS = QH // KVH
RESP = 256
CTX = 288
PROMPT = CTX - RESP
RANK = 64
FEATS = 896
FACTOR = 1.0 / math.sqrt(HD)
LOG2E = math.log2(math.e)
adapter_scale = 2.0

NX, NZ, NC, NY = 4, 8, 2, 8
HALF = CTX // 2
ROWS = 16

FAR_FIRST = (4, 3, 5, 2, 6, 1, 7)

RB = 128
SEEN = (PROMPT + RB, CTX)

VMEM_LIMIT = 60 * 1024 * 1024

NT = (((1,), (1,)), ((), ()))


def dot(a, b):
    return jnp.dot(a, b, preferred_element_type=F32)


def dot_nt(a, b):
    return lax.dot_general(a, b, NT, preferred_element_type=F32)


def rows_of_heads(ref, b):
    return jnp.concatenate(
        [ref[b * RB : (b + 1) * RB, h * HD : (h + 1) * HD] for h in range(HEADS)], axis=0
    )


def kernel(
    x_hbm, q_hbm, k_hbm, v_hbm, g_hbm, mask_hbm, length_hbm, w_hbm, at_hbm, b_hbm,
    lig_hbm, qg_hbm, kg_hbm, sums_hbm,
    x_ref, q_ref, k_ref, v_ref, g_ref, at_ref, mask_ref, length_ref,
    b_ref, wfull, vgfull,
    p0, p1, pb0, pb1,
    down_out, down_in, downs, ups,
    rs_src, rs_dst, bc_buf, total_ref,
    lig_ref, qg_ref, kg_ref,
    load_sem, store_sem, w1_send, w1_recv, wz_send, wz_recv, wx_send, wx_recv, wc_send, wc_recv,
    d1_send, d1_recv, d2_send, d2_recv, up_send, up_recv, vg_send, vg_recv,
    rs_send, rs_recv, bc_send, bc_recv, ag_send, ag_recv,
):
    dp = lax.axis_index("dp")
    y = lax.axis_index("tp")
    x = dp // (NZ * NC)
    z = (dp // NC) % NZ
    c = dp % NC

    def at(px, pz, pc, py):
        return {"dp": (px * NZ + pz) * NC + pc, "tp": py}

    y_to = [(y + k) % NY for k in FAR_FIRST]
    y_from = [(y + NY - k) % NY for k in FAR_FIRST]
    z_to = [(z + k) % NZ for k in FAR_FIRST]
    z_from = [(z + NZ - k) % NZ for k in FAR_FIRST]
    x_to = [(x + k) % NX for k in (2, 1, 3)]
    x_from = [(x + NX - k) % NX for k in (2, 1, 3)]
    xc_steps = [(i, j) for i in (2, 1, 3, 0) for j in (1, 0) if i or j]
    xc_to = [((x + i) % NX, (c + j) % NC) for i, j in xc_steps]
    xc_from = [((x + NX - i) % NX, (c + NC - j) % NC) for i, j in xc_steps]
    y_dev = [at(x, z, c, j) for j in y_to]
    z_dev = [at(x, j, c, y) for j in z_to]
    x_dev = [at(j, z, c, y) for j in x_to]
    xc_dev = [at(i, z, j, y) for i, j in xc_to]
    sibling = at(x, z, 1 - c, y)

    def remote(src, dst, send, recv, device):
        return pltpu.make_async_remote_copy(
            src_ref=src, dst_ref=dst, send_sem=send, recv_sem=recv, device_id=device, device_id_type=MESH
        )

    pending = []
    stores = [
        pltpu.make_async_copy(src, dst, store_sem.at[i])
        for i, (src, dst) in enumerate(
            [(lig_ref, lig_hbm), (qg_ref, qg_hbm), (kg_ref, kg_hbm), (total_ref, sums_hbm.at[z])]
        )
    ]

    def fan_out(src, dst, send, recv, devices):
        for k, device in enumerate(devices):
            copy = remote(src(k), dst, send.at[k], recv.at[k], device)
            copy.start()
            pending.append(copy)

    def landed(dst, send, recv, devices):
        for k, device in enumerate(devices):
            remote(dst(k), dst(k), send.at[k], recv.at[k], device).wait_recv()

    barrier = pltpu.get_barrier_semaphore()
    everyone = y_dev + z_dev + xc_dev
    for device in everyone:
        pl.semaphore_signal(barrier, inc=1, device_id=device, device_id_type=MESH)

    w_y = 4 * c + x
    w_rows = pl.ds(pl.multiple_of(z * ROWS, ROWS), ROWS)

    def w_cols(j):
        return pl.ds(pl.multiple_of(j * FEATS, 128), FEATS)

    loads = [
        pltpu.make_async_copy(src, dst, load_sem.at[i])
        for i, (src, dst) in enumerate(
            [
                (x_hbm, x_ref),
                (at_hbm, at_ref),
                (k_hbm, k_ref),
                (q_hbm, q_ref),
                (g_hbm, g_ref),
                (v_hbm, v_ref),
                (b_hbm, b_ref),
                (mask_hbm, mask_ref),
                (length_hbm, length_ref),
            ]
        )
    ]
    for load in loads:
        load.start()
    load_x, load_a, load_k, load_q, load_g, load_v, load_b, load_mask, load_length = loads
    w_own = pltpu.make_async_copy(w_hbm.at[w_rows, w_cols(y)], wfull.at[w_y, z], load_sem.at[9])

    @pl.when(y == w_y)
    def _():
        w_own.start()

    def first(factor):
        return jnp.concatenate([factor, jnp.zeros_like(factor)], axis=0)

    def second(factor):
        return jnp.concatenate([jnp.zeros_like(factor), factor], axis=0)

    def rank_rows(rows, factor):
        return dot_nt(rows[:HALF], first(factor)) + dot_nt(rows[HALF:], second(factor))

    def over_tokens(pairs, rows):
        pairs_t = pairs.T.astype(BF16)
        return dot(pairs_t, rows[:HALF])[:RANK] + dot(pairs_t, rows[HALF:])[RANK:]

    def sum_of(parts):
        total = parts[0].astype(F32)
        for j in range(1, parts.shape[0]):
            total = total + parts[j].astype(F32)
        return total

    load_x.wait()
    load_a.wait()
    down = rank_rows(x_ref, at_ref[...]).astype(BF16)
    for j in range(NY):
        down_out[j, 0] = down[j * ROWS : (j + 1) * ROWS]
        down_out[j, 1] = down[NY * ROWS :]

    load_k.wait()
    load_q.wait()
    load_mask.wait()
    load_length.wait()
    limit = PROMPT - 1 + length_ref[0]
    probs = (p0, p1)
    probs_low = (pb0, pb1)

    def weigh(b, h):
        seen = SEEN[b]
        q = q_ref[b * RB : (b + 1) * RB, h * HD : (h + 1) * HD]
        scores = dot_nt(k_ref[:seen, :], q) * (FACTOR * LOG2E)
        col = lax.broadcasted_iota(jnp.int32, (seen, RB), 0)
        row = lax.broadcasted_iota(jnp.int32, (1, RB), 1) + b * RB
        last = jnp.minimum(row + PROMPT, limit)
        scores = jnp.where(col <= last, scores, -1e30)
        top = jnp.max(scores, axis=0, keepdims=True)
        expo = jnp.exp2(scores - top)
        keep = jnp.where(row + PROMPT <= limit, mask_ref[:, b * RB : (b + 1) * RB], 0).astype(F32)
        p = expo * (keep / jnp.sum(expo, axis=0, keepdims=True))
        probs[b][:, h * HD : (h + 1) * HD] = p
        probs_low[b][:, h * HD : (h + 1) * HD] = p.astype(BF16)

    for h in range(HEADS):
        for b in range(2):
            weigh(b, h)

    load_g.wait()
    early = dot(pb0[...], rows_of_heads(g_ref, 0))
    late = dot(pb1[...], rows_of_heads(g_ref, 1))
    vgfull[y, : SEEN[0], :] = (early + late[: SEEN[0]]).astype(BF16)
    vgfull[y, SEEN[0] :, :] = late[SEEN[0] :].astype(BF16)
    load_b.wait()
    own_values = vgfull[y]
    ups[y] = rank_rows(own_values, b_ref[...]).astype(BF16)

    pl.semaphore_wait(barrier, len(everyone))

    @pl.when(y == w_y)
    def _():
        for k in range(NY - 1):
            remote(
                w_hbm.at[w_rows, w_cols(y_to[k])], wfull.at[w_y, z], w1_send.at[k], w1_recv, y_dev[k]
            ).start()

    fan_out(lambda k: down_out.at[y_to[k]], down_in.at[y], d1_send, d1_recv, y_dev)
    fan_out(lambda k: ups.at[y], ups.at[y], up_send, up_recv, y_dev)

    load_v.wait()
    for h in range(HEADS):
        for b in range(2):
            seen = SEEN[b]
            lanes = slice(h * HD, (h + 1) * HD)
            p = probs[b][:, lanes]
            t = p * dot_nt(v_ref[:seen, :], g_ref[b * RB : (b + 1) * RB, lanes])
            probs_low[b][:, lanes] = ((t - p * jnp.sum(t, axis=0, keepdims=True)) * FACTOR).astype(BF16)

    early = dot(pb0[...], rows_of_heads(q_ref, 0))
    late = dot(pb1[...], rows_of_heads(q_ref, 1))
    kg_ref[: SEEN[0], :] = (early + late[: SEEN[0]]).astype(BF16)
    kg_ref[SEEN[0] :, :] = late[SEEN[0] :].astype(BF16)
    keys_t = k_ref[...].astype(F32).T.astype(BF16)
    for b in range(2):
        qg_t = dot(keys_t[:, : SEEN[b]], probs_low[b][...])
        for h in range(HEADS):
            lanes = slice(h * HD, (h + 1) * HD)
            qg_ref[b * RB : (b + 1) * RB, lanes] = qg_t[:, lanes].T.astype(BF16)

    stores[1].start()
    stores[2].start()

    @pl.when(y == w_y)
    def _():
        w_own.wait()

    @pl.when(y != w_y)
    def _():
        remote(wfull.at[w_y, z], wfull.at[w_y, z], w1_send.at[0], w1_recv, y_dev[0]).wait_recv()

    fan_out(lambda k: wfull.at[w_y, z], wfull.at[w_y, z], wz_send, wz_recv, z_dev)

    landed(lambda k: down_in.at[y_from[k]], d1_send, d1_recv, y_dev)
    piece = down_out[y].astype(F32)
    for k in range(NY - 1):
        piece = piece + down_in[y_from[k]].astype(F32)
    downs[y] = piece[0].astype(BF16)
    fan_out(lambda k: downs.at[y], downs.at[y], d2_send, d2_recv, y_dev)

    def send_core(k, block):
        return remote(wfull.at[block], wfull.at[block], wc_send.at[k], wc_recv.at[k], sibling)

    def send_rs(k):
        return remote(rs_src.at[z_to[k]], rs_dst.at[z], rs_send.at[k], rs_recv.at[k], z_dev[k])

    landed(lambda k: wfull.at[w_y, z_from[k]], wz_send, wz_recv, z_dev)
    fan_out(lambda k: wfull.at[w_y], wfull.at[w_y], wx_send, wx_recv, x_dev)
    send_core(0, w_y).start()

    landed(lambda k: ups.at[y_from[k]], up_send, up_recv, y_dev)
    fan_out(lambda k: vgfull.at[y], vgfull.at[y], vg_send, vg_recv, y_dev)
    up = sum_of(ups)
    dfg_t = over_tokens(up, x_ref)
    for j in range(NZ - 1):
        rs_src[j] = dfg_t[:, j * 128 : (j + 1) * 128].astype(BF16)
    for k in range(NZ - 1):

        @pl.when(z_to[k] < NZ - 1)
        def _():
            send_rs(k).start()

    landed(lambda k: downs.at[y_from[k]], d2_send, d2_recv, y_dev)
    down = jnp.concatenate([downs[...].reshape(NY * ROWS, HD).astype(F32), piece[1]], axis=0)
    rs_src[NZ - 1] = over_tokens(down, own_values).astype(BF16)

    for k in range(NZ - 1):

        @pl.when(z_to[k] == NZ - 1)
        def _():
            send_rs(k).start()

    landed(lambda k: rs_dst.at[z_from[k]], rs_send, rs_recv, z_dev)
    total = rs_src[z].astype(F32)
    for k in range(NZ - 1):
        total = total + rs_dst[z_from[k]].astype(F32)
    bc_buf[x * NC + c] = total.astype(BF16)
    fan_out(lambda k: bc_buf.at[x * NC + c], bc_buf.at[x * NC + c], bc_send, bc_recv, xc_dev)

    landed(lambda k: bc_buf.at[xc_from[k][0] * NC + xc_from[k][1]], bc_send, bc_recv, xc_dev)
    total_ref[...] = sum_of(bc_buf).astype(BF16)
    stores[3].start()
    fan_out(lambda k: total_ref, sums_hbm.at[z], ag_send, ag_recv, z_dev)
    for k in range(NX - 1):
        remote(wfull.at[4 * c + x_from[k]], wfull.at[4 * c + x_from[k]], wx_send.at[k], wx_recv.at[k], x_dev[k]).wait_recv()
        send_core(1 + k, 4 * c + x_from[k]).start()

    landed(lambda k: vgfull.at[y_from[k]], vg_send, vg_recv, y_dev)
    send_core(0, 4 * (1 - c) + x).wait_recv()
    for k in range(NX - 1):
        send_core(1 + k, 4 * (1 - c) + x_from[k]).wait_recv()
    values = jnp.concatenate([vgfull[j] for j in range(NY)], axis=1)
    up = up.astype(BF16)
    for low, high in ((0, 256), (256, 512), (512, 768), (768, 896)):
        frozen = dot(values, wfull[:, :, :, low:high].reshape(NY * HD, high - low))
        down = at_ref[:, low:high]
        for rows, factor in ((slice(0, HALF), first(down)), (slice(HALF, CTX), second(down))):
            lig_ref[rows, low:high] = (frozen[rows] + adapter_scale * dot(up, factor)).astype(BF16)
    stores[0].start()

    landed(lambda k: sums_hbm.at[z_from[k]], ag_send, ag_recv, z_dev)

    for k in range(NZ - 1):
        send_rs(k).wait_send()
    send_core(0, w_y).wait_send()
    for k in range(NX - 1):
        send_core(1 + k, 4 * c + x_from[k]).wait_send()
    for copy in pending:
        copy.wait_send()
    for store in stores:
        store.wait()

    @pl.when(y == w_y)
    def _():
        for k in range(NY - 1):
            remote(
                w_hbm.at[w_rows, w_cols(y_to[k])], wfull.at[w_y, z], w1_send.at[k], w1_recv, y_dev[k]
            ).wait_send()


def hand_on(
    lig_hbm, qg_hbm, kg_hbm, sums_hbm,
    lig_out, qg_out, kg_out, dfg_out, ufg_out,
    lig, qg, kg, sums, dfg, ufg, sems,
):
    ins = [
        pltpu.make_async_copy(src, via, sems.at[i])
        for i, (src, via) in enumerate([(sums_hbm, sums), (lig_hbm, lig), (qg_hbm, qg), (kg_hbm, kg)])
    ]
    outs = [
        pltpu.make_async_copy(via, dst, sems.at[4 + i])
        for i, (via, dst) in enumerate([(lig, lig_out), (qg, qg_out), (kg, kg_out), (dfg, dfg_out), (ufg, ufg_out)])
    ]
    for copy in ins:
        copy.start()
    for i in range(3):
        ins[i + 1].wait()
        outs[i].start()
    ins[0].wait()
    for j in range(NZ - 1):
        dfg[:, j * 128 : (j + 1) * 128] = adapter_scale * sums[j].astype(F32)
    outs[3].start()
    ufg[...] = adapter_scale * sums[NZ - 1].astype(F32)
    outs[4].start()
    for copy in outs:
        copy.wait()


def per_device(
    normed_layer_input,
    queries,
    saved_key_rows,
    saved_value_rows,
    attention_output_gradient,
    finisher_token_mask,
    response_length,
    value_weight_matrix,
    adapter_down_factor,
    adapter_up_factor,
):
    hbm = pl.BlockSpec(memory_space=pltpu.HBM)
    dma = pltpu.SemaphoreType.DMA
    outs = pl.pallas_call(
        kernel,
        out_shape=(
            jax.ShapeDtypeStruct((CTX, FEATS), BF16),
            jax.ShapeDtypeStruct((RESP, FEATS), BF16),
            jax.ShapeDtypeStruct((CTX, HD), BF16),
            jax.ShapeDtypeStruct((NZ, RANK, HD), BF16),
        ),
        in_specs=[hbm] * 10,
        out_specs=(hbm,) * 4,
        scratch_shapes=[
            pltpu.VMEM((CTX, FEATS), BF16),
            pltpu.VMEM((RESP, FEATS), BF16),
            pltpu.VMEM((CTX, HD), BF16),
            pltpu.VMEM((CTX, HD), BF16),
            pltpu.VMEM((RESP, FEATS), BF16),
            pltpu.VMEM((RANK, FEATS), BF16),
            pltpu.VMEM((1, RESP), jnp.int32),
            pltpu.SMEM((1,), jnp.int32),
            pltpu.VMEM((RANK, HD), BF16),
            pltpu.VMEM((NY, NZ, ROWS, FEATS), BF16),
            pltpu.VMEM((NY, CTX, HD), BF16),
            pltpu.VMEM((SEEN[0], FEATS), F32),
            pltpu.VMEM((SEEN[1], FEATS), F32),
            pltpu.VMEM((SEEN[0], FEATS), BF16),
            pltpu.VMEM((SEEN[1], FEATS), BF16),
            pltpu.VMEM((NY, 2, ROWS, HD), BF16),
            pltpu.VMEM((NY, 2, ROWS, HD), BF16),
            pltpu.VMEM((NY, ROWS, HD), BF16),
            pltpu.VMEM((NY, HALF, HD), BF16),
            pltpu.VMEM((NZ, RANK, HD), BF16),
            pltpu.VMEM((NZ, RANK, HD), BF16),
            pltpu.VMEM((NX * NC, RANK, HD), BF16),
            pltpu.VMEM((RANK, HD), BF16),
            pltpu.VMEM((CTX, FEATS), BF16),
            pltpu.VMEM((RESP, FEATS), BF16),
            pltpu.VMEM((CTX, HD), BF16),
            dma((10,)),
            dma((4,)),
            dma((NY - 1,)),
            dma,
            dma((NZ - 1,)),
            dma((NZ - 1,)),
            dma((NX - 1,)),
            dma((NX - 1,)),
            dma((NX,)),
            dma((NX,)),
            dma((NY - 1,)),
            dma((NY - 1,)),
            dma((NY - 1,)),
            dma((NY - 1,)),
            dma((NY - 1,)),
            dma((NY - 1,)),
            dma((NY - 1,)),
            dma((NY - 1,)),
            dma((NZ - 1,)),
            dma((NZ - 1,)),
            dma((NX * NC - 1,)),
            dma((NX * NC - 1,)),
            dma((NZ - 1,)),
            dma((NZ - 1,)),
        ],
        compiler_params=pltpu.CompilerParams(
            collective_id=0, has_side_effects=True, vmem_limit_bytes=VMEM_LIMIT
        ),
    )(
        normed_layer_input,
        queries,
        saved_key_rows,
        saved_value_rows,
        attention_output_gradient,
        finisher_token_mask.reshape(1, RESP),
        response_length,
        value_weight_matrix,
        adapter_down_factor.T,
        adapter_up_factor,
    )
    lig, qg, kg, dfg_t, ufg = pl.pallas_call(
        hand_on,
        out_shape=(
            jax.ShapeDtypeStruct((CTX, FEATS), BF16),
            jax.ShapeDtypeStruct((RESP, FEATS), BF16),
            jax.ShapeDtypeStruct((CTX, HD), BF16),
            jax.ShapeDtypeStruct((RANK, FEATS), F32),
            jax.ShapeDtypeStruct((RANK, HD), F32),
        ),
        in_specs=[hbm] * 4,
        out_specs=(hbm,) * 5,
        scratch_shapes=[
            pltpu.VMEM((CTX, FEATS), BF16),
            pltpu.VMEM((RESP, FEATS), BF16),
            pltpu.VMEM((CTX, HD), BF16),
            pltpu.VMEM((NZ, RANK, HD), BF16),
            pltpu.VMEM((RANK, FEATS), F32),
            pltpu.VMEM((RANK, HD), F32),
            dma((9,)),
        ],
        compiler_params=pltpu.CompilerParams(vmem_limit_bytes=VMEM_LIMIT),
    )(*outs)
    return (lig, qg, kg, dfg_t.T, ufg)


def solution(mesh):
    in_specs = (
        P("dp", "tp"),
        P("dp", "tp"),
        P("dp", "tp"),
        P("dp", "tp"),
        P("dp", "tp"),
        P("dp"),
        P("dp"),
        P("tp", None),
        P("tp", None),
        P(None, "tp"),
    )
    out_specs = (P("dp", "tp"), P("dp", "tp"), P("dp", "tp"), P("tp", None), P(None, "tp"))
    return jax.shard_map(
        per_device, mesh=mesh, in_specs=in_specs, out_specs=out_specs, check_vma=False
    )
```

```python
import math

import jax
import jax.numpy as jnp
from jax import lax
from jax.experimental import pallas as pl
from jax.experimental.pallas import tpu as pltpu
from jax.sharding import PartitionSpec as P

MESH = pl.DeviceIdType.MESH
BF16 = jnp.bfloat16
F32 = jnp.float32

QH = 56
KVH = 8
HD = 128
HEADS = QH // KVH
RESP = 256
CTX = 288
PROMPT = CTX - RESP
RANK = 64
FEATS = 896
FACTOR = 1.0 / math.sqrt(HD)
LOG2E = math.log2(math.e)
adapter_scale = 2.0

NX, NZ, NC, NY = 4, 8, 2, 8
HALF = CTX // 2
ROWS = 16

FAR_FIRST = (4, 3, 5, 2, 6, 1, 7)

RB = 128
SEEN = (PROMPT + RB, CTX)

VMEM_LIMIT = 60 * 1024 * 1024

NT = (((1,), (1,)), ((), ()))


def dot(a, b):
    return jnp.dot(a, b, preferred_element_type=F32)


def dot_nt(a, b):
    return lax.dot_general(a, b, NT, preferred_element_type=F32)


def rows_of_heads(ref, b):
    return jnp.concatenate(
        [ref[b * RB : (b + 1) * RB, h * HD : (h + 1) * HD] for h in range(HEADS)], axis=0
    )


def kernel(
    x_hbm, q_hbm, k_hbm, v_hbm, g_hbm, mask_hbm, length_hbm, w_hbm, at_hbm, b_hbm,
    lig_hbm, qg_hbm, kg_hbm, sums_hbm,
    x_ref, q_ref, k_ref, v_ref, g_ref, at_ref, mask_ref, length_ref,
    b_ref, wfull, vgfull,
    p0, p1, pb0, pb1,
    parts_out, parts_in, sums,
    rs_src, rs_dst, bc_buf, total_ref,
    lig_ref, qg_ref, kg_ref,
    load_sem, store_sem, w1_send, w1_recv, wz_send, wz_recv, wx_send, wx_recv, wc_send, wc_recv,
    d1_send, d1_recv, d2_send, d2_recv, vg_send, vg_recv,
    rs_send, rs_recv, bc_send, bc_recv, ag_send, ag_recv,
):
    dp = lax.axis_index("dp")
    y = lax.axis_index("tp")
    x = dp // (NZ * NC)
    z = (dp // NC) % NZ
    c = dp % NC

    def at(px, pz, pc, py):
        return {"dp": (px * NZ + pz) * NC + pc, "tp": py}

    y_to = [(y + k) % NY for k in FAR_FIRST]
    y_from = [(y + NY - k) % NY for k in FAR_FIRST]
    z_to = [(z + k) % NZ for k in FAR_FIRST]
    z_from = [(z + NZ - k) % NZ for k in FAR_FIRST]
    x_to = [(x + k) % NX for k in (2, 1, 3)]
    x_from = [(x + NX - k) % NX for k in (2, 1, 3)]
    xc_steps = [(i, j) for i in (2, 1, 3, 0) for j in (1, 0) if i or j]
    xc_to = [((x + i) % NX, (c + j) % NC) for i, j in xc_steps]
    xc_from = [((x + NX - i) % NX, (c + NC - j) % NC) for i, j in xc_steps]
    y_dev = [at(x, z, c, j) for j in y_to]
    z_dev = [at(x, j, c, y) for j in z_to]
    x_dev = [at(j, z, c, y) for j in x_to]
    xc_dev = [at(i, z, j, y) for i, j in xc_to]
    sibling = at(x, z, 1 - c, y)

    def remote(src, dst, send, recv, device):
        return pltpu.make_async_remote_copy(
            src_ref=src, dst_ref=dst, send_sem=send, recv_sem=recv, device_id=device, device_id_type=MESH
        )

    pending = []
    stores = [
        pltpu.make_async_copy(src, dst, store_sem.at[i])
        for i, (src, dst) in enumerate(
            [(lig_ref, lig_hbm), (qg_ref, qg_hbm), (kg_ref, kg_hbm), (total_ref, sums_hbm.at[z])]
        )
    ]

    def fan_out(src, dst, send, recv, devices):
        for k, device in enumerate(devices):
            copy = remote(src(k), dst, send.at[k], recv.at[k], device)
            copy.start()
            pending.append(copy)

    def landed(dst, send, recv, devices):
        for k, device in enumerate(devices):
            remote(dst(k), dst(k), send.at[k], recv.at[k], device).wait_recv()

    w_y = 4 * c + x
    w_rows = pl.ds(pl.multiple_of(z * ROWS, ROWS), ROWS)

    def w_cols(j):
        return pl.ds(pl.multiple_of(j * FEATS, 128), FEATS)

    loads = [
        pltpu.make_async_copy(src, dst, load_sem.at[i])
        for i, (src, dst) in enumerate(
            [
                (k_hbm, k_ref),
                (q_hbm, q_ref),
                (x_hbm, x_ref),
                (at_hbm, at_ref),
                (g_hbm, g_ref),
                (v_hbm, v_ref),
                (b_hbm, b_ref),
                (mask_hbm, mask_ref),
                (length_hbm, length_ref),
            ]
        )
    ]
    for load in loads:
        load.start()
    barrier = pltpu.get_barrier_semaphore()
    everyone = y_dev + z_dev + xc_dev
    for device in everyone:
        pl.semaphore_signal(barrier, inc=1, device_id=device, device_id_type=MESH)

    load_k, load_q, load_x, load_a, load_g, load_v, load_b, load_mask, load_length = loads
    w_own = pltpu.make_async_copy(w_hbm.at[w_rows, w_cols(y)], wfull.at[w_y, z], load_sem.at[9])

    @pl.when(y == w_y)
    def _():
        w_own.start()

    def first(factor):
        return jnp.concatenate([factor, jnp.zeros_like(factor)], axis=0)

    def second(factor):
        return jnp.concatenate([jnp.zeros_like(factor), factor], axis=0)

    def rank_rows(rows, factor):
        return dot_nt(rows[:HALF], first(factor)) + dot_nt(rows[HALF:], second(factor))

    def over_tokens(pairs, rows):
        pairs_t = pairs.T.astype(BF16)
        return dot(pairs_t, rows[:HALF])[:RANK] + dot(pairs_t, rows[HALF:])[RANK:]

    def sum_of(parts):
        total = parts[0].astype(F32)
        for j in range(1, parts.shape[0]):
            total = total + parts[j].astype(F32)
        return total

    load_k.wait()
    load_q.wait()
    load_mask.wait()
    load_length.wait()
    limit = PROMPT - 1 + length_ref[0]
    probs = (p0, p1)
    probs_low = (pb0, pb1)

    def weigh(b, h):
        seen = SEEN[b]
        q = q_ref[b * RB : (b + 1) * RB, h * HD : (h + 1) * HD]
        scores = dot_nt(k_ref[:seen, :], q) * (FACTOR * LOG2E)
        col = lax.broadcasted_iota(jnp.int32, (seen, RB), 0)
        row = lax.broadcasted_iota(jnp.int32, (1, RB), 1) + b * RB
        last = jnp.minimum(row + PROMPT, limit)
        scores = jnp.where(col <= last, scores, -1e30)
        top = jnp.max(scores, axis=0, keepdims=True)
        expo = jnp.exp2(scores - top)
        keep = jnp.where(row + PROMPT <= limit, mask_ref[:, b * RB : (b + 1) * RB], 0).astype(F32)
        p = expo * (keep / jnp.sum(expo, axis=0, keepdims=True))
        probs[b][:, h * HD : (h + 1) * HD] = p
        probs_low[b][:, h * HD : (h + 1) * HD] = p.astype(BF16)

    for h in range(HEADS):
        for b in range(2):
            weigh(b, h)

    def hand_out(i, rows):
        rows = rows.astype(BF16)
        for j in range(NY):
            parts_out[j, i] = rows[j * ROWS : (j + 1) * ROWS]
            parts_out[j, 2 + i] = rows[NY * ROWS :]

    load_x.wait()
    load_a.wait()
    hand_out(0, rank_rows(x_ref, at_ref[...]))
    load_g.wait()
    early = dot(pb0[...], rows_of_heads(g_ref, 0))
    late = dot(pb1[...], rows_of_heads(g_ref, 1))
    vgfull[y, : SEEN[0], :] = (early + late[: SEEN[0]]).astype(BF16)
    vgfull[y, SEEN[0] :, :] = late[SEEN[0] :].astype(BF16)
    load_b.wait()
    own_values = vgfull[y]
    hand_out(1, rank_rows(own_values, b_ref[...]))

    pl.semaphore_wait(barrier, len(everyone))

    @pl.when(y == w_y)
    def _():
        for k in range(NY - 1):
            remote(
                w_hbm.at[w_rows, w_cols(y_to[k])], wfull.at[w_y, z], w1_send.at[k], w1_recv, y_dev[k]
            ).start()

    fan_out(lambda k: parts_out.at[y_to[k]], parts_in.at[y], d1_send, d1_recv, y_dev)

    load_v.wait()
    for h in range(HEADS):
        for b in range(2):
            seen = SEEN[b]
            lanes = slice(h * HD, (h + 1) * HD)
            p = probs[b][:, lanes]
            t = p * dot_nt(v_ref[:seen, :], g_ref[b * RB : (b + 1) * RB, lanes])
            probs_low[b][:, lanes] = ((t - p * jnp.sum(t, axis=0, keepdims=True)) * FACTOR).astype(BF16)

    early = dot(pb0[...], rows_of_heads(q_ref, 0))
    late = dot(pb1[...], rows_of_heads(q_ref, 1))
    kg_ref[: SEEN[0], :] = (early + late[: SEEN[0]]).astype(BF16)
    kg_ref[SEEN[0] :, :] = late[SEEN[0] :].astype(BF16)
    keys_t = k_ref[...].astype(F32).T.astype(BF16)
    for b in range(2):
        qg_t = dot(keys_t[:, : SEEN[b]], probs_low[b][...])
        for h in range(HEADS):
            lanes = slice(h * HD, (h + 1) * HD)
            qg_ref[b * RB : (b + 1) * RB, lanes] = qg_t[:, lanes].T.astype(BF16)

    stores[1].start()
    stores[2].start()

    @pl.when(y == w_y)
    def _():
        w_own.wait()

    @pl.when(y != w_y)
    def _():
        remote(wfull.at[w_y, z], wfull.at[w_y, z], w1_send.at[0], w1_recv, y_dev[0]).wait_recv()

    fan_out(lambda k: wfull.at[w_y, z], wfull.at[w_y, z], wz_send, wz_recv, z_dev)

    landed(lambda k: parts_in.at[y_from[k]], d1_send, d1_recv, y_dev)
    total_rows = parts_out[y].astype(F32)
    for k in range(NY - 1):
        total_rows = total_rows + parts_in[y_from[k]].astype(F32)
    sums[y] = total_rows[:2].astype(BF16)
    fan_out(lambda k: sums.at[y], sums.at[y], d2_send, d2_recv, y_dev)

    def summed(i):
        return jnp.concatenate([sums[:, i].reshape(NY * ROWS, HD).astype(F32), total_rows[2 + i]], axis=0)

    def first_half(block):
        return wfull.at[block, : NZ // 2]

    def second_half(block):
        return wfull.at[block, NZ // 2 :]

    def send_core(k, block):
        return remote(wfull.at[block], wfull.at[block], wc_send.at[k], wc_recv.at[k], sibling)

    landed(lambda k: sums.at[y_from[k]], d2_send, d2_recv, y_dev)
    fan_out(lambda k: vgfull.at[y], vgfull.at[y], vg_send, vg_recv, y_dev)
    up = summed(1)
    dfg_t = over_tokens(up, x_ref)
    for j in range(NZ - 1):
        rs_src[j] = dfg_t[:, j * 128 : (j + 1) * 128].astype(BF16)
    rs_src[NZ - 1] = over_tokens(summed(0), own_values).astype(BF16)
    fan_out(lambda k: rs_src.at[z_to[k]], rs_dst.at[z], rs_send, rs_recv, z_dev)

    landed(lambda k: wfull.at[w_y, z_from[k]], wz_send, wz_recv, z_dev)
    fan_out(lambda k: first_half(w_y), first_half(w_y), wx_send.at[0], wx_recv.at[0], x_dev)
    send_core(0, w_y).start()

    landed(lambda k: rs_dst.at[z_from[k]], rs_send, rs_recv, z_dev)
    total = rs_src[z].astype(F32)
    for k in range(NZ - 1):
        total = total + rs_dst[z_from[k]].astype(F32)
    bc_buf[x * NC + c] = total.astype(BF16)
    fan_out(lambda k: bc_buf.at[x * NC + c], bc_buf.at[x * NC + c], bc_send, bc_recv, xc_dev)
    fan_out(lambda k: second_half(w_y), second_half(w_y), wx_send.at[1], wx_recv.at[1], x_dev)

    landed(lambda k: bc_buf.at[xc_from[k][0] * NC + xc_from[k][1]], bc_send, bc_recv, xc_dev)
    total_ref[...] = sum_of(bc_buf).astype(BF16)
    stores[3].start()
    fan_out(lambda k: total_ref, sums_hbm.at[z], ag_send, ag_recv, z_dev)
    for k in range(NX - 1):
        block = 4 * c + x_from[k]
        for i, half in enumerate((first_half(block), second_half(block))):
            remote(half, half, wx_send.at[i, k], wx_recv.at[i, k], x_dev[k]).wait_recv()
        send_core(1 + k, block).start()

    landed(lambda k: vgfull.at[y_from[k]], vg_send, vg_recv, y_dev)
    send_core(0, 4 * (1 - c) + x).wait_recv()
    for k in range(NX - 1):
        send_core(1 + k, 4 * (1 - c) + x_from[k]).wait_recv()
    values = jnp.concatenate([vgfull[j] for j in range(NY)], axis=1)
    up = up.astype(BF16)
    for low, high in ((0, 256), (256, 512), (512, 768), (768, 896)):
        frozen = dot(values, wfull[:, :, :, low:high].reshape(NY * HD, high - low))
        down = at_ref[:, low:high]
        for rows, factor in ((slice(0, HALF), first(down)), (slice(HALF, CTX), second(down))):
            lig_ref[rows, low:high] = (frozen[rows] + adapter_scale * dot(up, factor)).astype(BF16)
    stores[0].start()

    landed(lambda k: sums_hbm.at[z_from[k]], ag_send, ag_recv, z_dev)

    send_core(0, w_y).wait_send()
    for k in range(NX - 1):
        send_core(1 + k, 4 * c + x_from[k]).wait_send()
    for copy in pending:
        copy.wait_send()
    for store in stores:
        store.wait()

    @pl.when(y == w_y)
    def _():
        for k in range(NY - 1):
            remote(
                w_hbm.at[w_rows, w_cols(y_to[k])], wfull.at[w_y, z], w1_send.at[k], w1_recv, y_dev[k]
            ).wait_send()


def hand_on(
    lig_hbm, qg_hbm, kg_hbm, sums_hbm,
    lig_out, qg_out, kg_out, dfg_out, ufg_out,
    lig, qg, kg, sums, dfg, ufg, in_sems, out_sems,
):
    pieces = [(sums_hbm, sums, None)]
    for src, via, dst, step in ((lig_hbm, lig, lig_out, 96), (qg_hbm, qg, qg_out, 64), (kg_hbm, kg, kg_out, CTX)):
        for low in range(0, src.shape[0], step):
            rows = pl.ds(low, step)
            pieces.append((src.at[rows], via.at[rows], dst.at[rows]))
    ins = [pltpu.make_async_copy(src, via, in_sems.at[i]) for i, (src, via, _) in enumerate(pieces)]
    outs = [pltpu.make_async_copy(via, dst, out_sems.at[i]) for i, (_, via, dst) in enumerate(pieces[1:])]
    outs += [
        pltpu.make_async_copy(via, dst, out_sems.at[len(outs) + i])
        for i, (via, dst) in enumerate([(dfg, dfg_out), (ufg, ufg_out)])
    ]
    for copy in ins:
        copy.start()
    ins[0].wait()
    for j in range(NZ - 1):
        dfg[:, j * 128 : (j + 1) * 128] = adapter_scale * sums[j].astype(F32)
    ufg[...] = adapter_scale * sums[NZ - 1].astype(F32)
    outs[-2].start()
    outs[-1].start()
    for before, after in zip(ins[1:], outs):
        before.wait()
        after.start()
    for copy in outs:
        copy.wait()


def per_device(
    normed_layer_input,
    queries,
    saved_key_rows,
    saved_value_rows,
    attention_output_gradient,
    finisher_token_mask,
    response_length,
    value_weight_matrix,
    adapter_down_factor,
    adapter_up_factor,
):
    hbm = pl.BlockSpec(memory_space=pltpu.HBM)
    dma = pltpu.SemaphoreType.DMA
    outs = pl.pallas_call(
        kernel,
        out_shape=(
            jax.ShapeDtypeStruct((CTX, FEATS), BF16),
            jax.ShapeDtypeStruct((RESP, FEATS), BF16),
            jax.ShapeDtypeStruct((CTX, HD), BF16),
            jax.ShapeDtypeStruct((NZ, RANK, HD), BF16),
        ),
        in_specs=[hbm] * 10,
        out_specs=(hbm,) * 4,
        scratch_shapes=[
            pltpu.VMEM((CTX, FEATS), BF16),
            pltpu.VMEM((RESP, FEATS), BF16),
            pltpu.VMEM((CTX, HD), BF16),
            pltpu.VMEM((CTX, HD), BF16),
            pltpu.VMEM((RESP, FEATS), BF16),
            pltpu.VMEM((RANK, FEATS), BF16),
            pltpu.VMEM((1, RESP), jnp.int32),
            pltpu.SMEM((1,), jnp.int32),
            pltpu.VMEM((RANK, HD), BF16),
            pltpu.VMEM((NY, NZ, ROWS, FEATS), BF16),
            pltpu.VMEM((NY, CTX, HD), BF16),
            pltpu.VMEM((SEEN[0], FEATS), F32),
            pltpu.VMEM((SEEN[1], FEATS), F32),
            pltpu.VMEM((SEEN[0], FEATS), BF16),
            pltpu.VMEM((SEEN[1], FEATS), BF16),
            pltpu.VMEM((NY, 4, ROWS, HD), BF16),
            pltpu.VMEM((NY, 4, ROWS, HD), BF16),
            pltpu.VMEM((NY, 2, ROWS, HD), BF16),
            pltpu.VMEM((NZ, RANK, HD), BF16),
            pltpu.VMEM((NZ, RANK, HD), BF16),
            pltpu.VMEM((NX * NC, RANK, HD), BF16),
            pltpu.VMEM((RANK, HD), BF16),
            pltpu.VMEM((CTX, FEATS), BF16),
            pltpu.VMEM((RESP, FEATS), BF16),
            pltpu.VMEM((CTX, HD), BF16),
            dma((10,)),
            dma((4,)),
            dma((NY - 1,)),
            dma,
            dma((NZ - 1,)),
            dma((NZ - 1,)),
            dma((2, NX - 1)),
            dma((2, NX - 1)),
            dma((NX,)),
            dma((NX,)),
            dma((NY - 1,)),
            dma((NY - 1,)),
            dma((NY - 1,)),
            dma((NY - 1,)),
            dma((NY - 1,)),
            dma((NY - 1,)),
            dma((NZ - 1,)),
            dma((NZ - 1,)),
            dma((NX * NC - 1,)),
            dma((NX * NC - 1,)),
            dma((NZ - 1,)),
            dma((NZ - 1,)),
        ],
        compiler_params=pltpu.CompilerParams(
            collective_id=0, has_side_effects=True, vmem_limit_bytes=VMEM_LIMIT
        ),
    )(
        normed_layer_input,
        queries,
        saved_key_rows,
        saved_value_rows,
        attention_output_gradient,
        finisher_token_mask.reshape(1, RESP),
        response_length,
        value_weight_matrix,
        adapter_down_factor.T,
        adapter_up_factor,
    )
    lig, qg, kg, dfg_t, ufg = pl.pallas_call(
        hand_on,
        out_shape=(
            jax.ShapeDtypeStruct((CTX, FEATS), BF16),
            jax.ShapeDtypeStruct((RESP, FEATS), BF16),
            jax.ShapeDtypeStruct((CTX, HD), BF16),
            jax.ShapeDtypeStruct((RANK, FEATS), F32),
            jax.ShapeDtypeStruct((RANK, HD), F32),
        ),
        in_specs=[hbm] * 4,
        out_specs=(hbm,) * 5,
        scratch_shapes=[
            pltpu.VMEM((CTX, FEATS), BF16),
            pltpu.VMEM((RESP, FEATS), BF16),
            pltpu.VMEM((CTX, HD), BF16),
            pltpu.VMEM((NZ, RANK, HD), BF16),
            pltpu.VMEM((RANK, FEATS), F32),
            pltpu.VMEM((RANK, HD), F32),
            dma((9,)),
            dma((10,)),
        ],
        compiler_params=pltpu.CompilerParams(vmem_limit_bytes=VMEM_LIMIT),
    )(*outs)
    return (lig, qg, kg, dfg_t.T, ufg)


def solution(mesh):
    in_specs = (
        P("dp", "tp"),
        P("dp", "tp"),
        P("dp", "tp"),
        P("dp", "tp"),
        P("dp", "tp"),
        P("dp"),
        P("dp"),
        P("tp", None),
        P("tp", None),
        P(None, "tp"),
    )
    out_specs = (P("dp", "tp"), P("dp", "tp"), P("dp", "tp"), P("tp", None), P(None, "tp"))
    return jax.shard_map(
        per_device, mesh=mesh, in_specs=in_specs, out_specs=out_specs, check_vma=False
    )
```

```python
import math

import jax
import jax.numpy as jnp
from jax import lax
from jax.experimental import pallas as pl
from jax.experimental.pallas import tpu as pltpu
from jax.sharding import PartitionSpec as P

MESH = pl.DeviceIdType.MESH
BF16 = jnp.bfloat16
F32 = jnp.float32

QH = 56
KVH = 8
HD = 128
HEADS = QH // KVH
RESP = 256
CTX = 288
PROMPT = CTX - RESP
RANK = 64
FEATS = 896
FACTOR = 1.0 / math.sqrt(HD)
LOG2E = math.log2(math.e)
adapter_scale = 2.0

NX, NZ, NC, NY = 4, 8, 2, 8
HALF = CTX // 2
ROWS = 16

WEIGHT_PARTS = ((0, 512), (512, 384))

FAR_FIRST = (4, 3, 5, 2, 6, 1, 7)

RB = 128
SEEN = (PROMPT + RB, CTX)

VMEM_LIMIT = 60 * 1024 * 1024

NT = (((1,), (1,)), ((), ()))


def dot(a, b):
    return jnp.dot(a, b, preferred_element_type=F32)


def dot_nt(a, b):
    return lax.dot_general(a, b, NT, preferred_element_type=F32)


def rows_of_heads(ref, b):
    return jnp.concatenate(
        [ref[b * RB : (b + 1) * RB, h * HD : (h + 1) * HD] for h in range(HEADS)], axis=0
    )


def kernel(
    x_hbm, q_hbm, k_hbm, v_hbm, g_hbm, mask_hbm, length_hbm, w_hbm, at_hbm, b_hbm,
    lig_hbm, qg_hbm, kg_hbm, sums_hbm,
    x_ref, q_ref, k_ref, v_ref, g_ref, at_ref, mask_ref, length_ref,
    b_ref, wfull, vgfull,
    p0, p1, pb0, pb1,
    parts_out, parts_in, sums,
    rs_src, rs_dst, bc_buf, total_ref,
    lig_ref, qg_ref, kg_ref,
    load_sem, store_sem, w1_send, w1_recv, wz_send, wz_recv, wx_send, wx_recv, wc_send, wc_recv,
    d1_send, d1_recv, d2_send, d2_recv, vg_send, vg_recv,
    rs_send, rs_recv, bc_send, bc_recv, ag_send, ag_recv,
):
    dp = lax.axis_index("dp")
    y = lax.axis_index("tp")
    x = dp // (NZ * NC)
    z = (dp // NC) % NZ
    c = dp % NC

    def at(px, pz, pc, py):
        return {"dp": (px * NZ + pz) * NC + pc, "tp": py}

    y_to = [(y + k) % NY for k in FAR_FIRST]
    y_from = [(y + NY - k) % NY for k in FAR_FIRST]
    z_to = [(z + k) % NZ for k in FAR_FIRST]
    z_from = [(z + NZ - k) % NZ for k in FAR_FIRST]
    x_to = [(x + k) % NX for k in (2, 1, 3)]
    x_from = [(x + NX - k) % NX for k in (2, 1, 3)]
    xc_steps = [(i, j) for i in (2, 1, 3, 0) for j in (1, 0) if i or j]
    xc_to = [((x + i) % NX, (c + j) % NC) for i, j in xc_steps]
    xc_from = [((x + NX - i) % NX, (c + NC - j) % NC) for i, j in xc_steps]
    y_dev = [at(x, z, c, j) for j in y_to]
    z_dev = [at(x, j, c, y) for j in z_to]
    x_dev = [at(j, z, c, y) for j in x_to]
    xc_dev = [at(i, z, j, y) for i, j in xc_to]
    sibling = at(x, z, 1 - c, y)

    def remote(src, dst, send, recv, device):
        return pltpu.make_async_remote_copy(
            src_ref=src, dst_ref=dst, send_sem=send, recv_sem=recv, device_id=device, device_id_type=MESH
        )

    pending = []
    stores = [
        pltpu.make_async_copy(src, dst, store_sem.at[i])
        for i, (src, dst) in enumerate(
            [(qg_ref, qg_hbm), (kg_ref, kg_hbm), (total_ref, sums_hbm.at[z])]
            + [(lig_ref.at[:, pl.ds(*cols)], lig_hbm.at[:, pl.ds(*cols)]) for cols in WEIGHT_PARTS]
        )
    ]

    def fan_out(src, dst, send, recv, devices):
        for k, device in enumerate(devices):
            copy = remote(src(k), dst, send.at[k], recv.at[k], device)
            copy.start()
            pending.append(copy)

    def landed(dst, send, recv, devices):
        for k, device in enumerate(devices):
            remote(dst(k), dst(k), send.at[k], recv.at[k], device).wait_recv()

    w_y = 4 * c + x
    w_rows = pl.ds(pl.multiple_of(z * ROWS, ROWS), ROWS)

    def w_cols(j):
        return pl.ds(pl.multiple_of(j * FEATS, 128), FEATS)

    loads = [
        pltpu.make_async_copy(src, dst, load_sem.at[i])
        for i, (src, dst) in enumerate(
            [
                (k_hbm, k_ref),
                (q_hbm, q_ref),
                (x_hbm, x_ref),
                (at_hbm, at_ref),
                (g_hbm, g_ref),
                (v_hbm, v_ref),
                (b_hbm, b_ref),
                (mask_hbm, mask_ref),
                (length_hbm, length_ref),
            ]
        )
    ]
    for load in loads:
        load.start()
    barrier = pltpu.get_barrier_semaphore()
    everyone = y_dev + z_dev + xc_dev
    for device in everyone:
        pl.semaphore_signal(barrier, inc=1, device_id=device, device_id_type=MESH)

    load_k, load_q, load_x, load_a, load_g, load_v, load_b, load_mask, load_length = loads
    w_own = pltpu.make_async_copy(w_hbm.at[w_rows, w_cols(y)], wfull.at[w_y, z], load_sem.at[9])

    @pl.when(y == w_y)
    def _():
        w_own.start()

    def first(factor):
        return jnp.concatenate([factor, jnp.zeros_like(factor)], axis=0)

    def second(factor):
        return jnp.concatenate([jnp.zeros_like(factor), factor], axis=0)

    def rank_rows(rows, factor):
        return dot_nt(rows[:HALF], first(factor)) + dot_nt(rows[HALF:], second(factor))

    def over_tokens(pairs, rows):
        pairs_t = pairs.T.astype(BF16)
        return dot(pairs_t, rows[:HALF])[:RANK] + dot(pairs_t, rows[HALF:])[RANK:]

    def sum_of(parts):
        total = parts[0].astype(F32)
        for j in range(1, parts.shape[0]):
            total = total + parts[j].astype(F32)
        return total

    load_k.wait()
    load_q.wait()
    load_mask.wait()
    load_length.wait()
    limit = PROMPT - 1 + length_ref[0]
    probs = (p0, p1)
    probs_low = (pb0, pb1)

    def weigh(b, h):
        seen = SEEN[b]
        q = q_ref[b * RB : (b + 1) * RB, h * HD : (h + 1) * HD]
        scores = dot_nt(k_ref[:seen, :], q) * (FACTOR * LOG2E)
        col = lax.broadcasted_iota(jnp.int32, (seen, RB), 0)
        row = lax.broadcasted_iota(jnp.int32, (1, RB), 1) + b * RB
        last = jnp.minimum(row + PROMPT, limit)
        scores = jnp.where(col <= last, scores, -1e30)
        top = jnp.max(scores, axis=0, keepdims=True)
        expo = jnp.exp2(scores - top)
        keep = jnp.where(row + PROMPT <= limit, mask_ref[:, b * RB : (b + 1) * RB], 0).astype(F32)
        p = expo * (keep / jnp.sum(expo, axis=0, keepdims=True))
        probs[b][:, h * HD : (h + 1) * HD] = p
        probs_low[b][:, h * HD : (h + 1) * HD] = p.astype(BF16)

    for h in range(HEADS):
        for b in range(2):
            weigh(b, h)

    def hand_out(i, rows):
        rows = rows.astype(BF16)
        for j in range(NY):
            parts_out[j, i] = rows[j * ROWS : (j + 1) * ROWS]
            parts_out[j, 2 + i] = rows[NY * ROWS :]

    load_x.wait()
    load_a.wait()
    hand_out(0, rank_rows(x_ref, at_ref[...]))
    load_g.wait()
    early = dot(pb0[...], rows_of_heads(g_ref, 0))
    late = dot(pb1[...], rows_of_heads(g_ref, 1))
    vgfull[y, : SEEN[0], :] = (early + late[: SEEN[0]]).astype(BF16)
    vgfull[y, SEEN[0] :, :] = late[SEEN[0] :].astype(BF16)
    load_b.wait()
    own_values = vgfull[y]
    hand_out(1, rank_rows(own_values, b_ref[...]))

    pl.semaphore_wait(barrier, len(everyone))

    fan_out(lambda k: parts_out.at[y_to[k]], parts_in.at[y], d1_send, d1_recv, y_dev)

    @pl.when(y == w_y)
    def _():
        for k in range(NY - 1):
            remote(
                w_hbm.at[w_rows, w_cols(y_to[k])], wfull.at[w_y, z], w1_send.at[k], w1_recv, y_dev[k]
            ).start()

    load_v.wait()
    for h in range(HEADS):
        for b in range(2):
            seen = SEEN[b]
            lanes = slice(h * HD, (h + 1) * HD)
            p = probs[b][:, lanes]
            t = p * dot_nt(v_ref[:seen, :], g_ref[b * RB : (b + 1) * RB, lanes])
            probs_low[b][:, lanes] = ((t - p * jnp.sum(t, axis=0, keepdims=True)) * FACTOR).astype(BF16)

    early = dot(pb0[...], rows_of_heads(q_ref, 0))
    late = dot(pb1[...], rows_of_heads(q_ref, 1))
    kg_ref[: SEEN[0], :] = (early + late[: SEEN[0]]).astype(BF16)
    kg_ref[SEEN[0] :, :] = late[SEEN[0] :].astype(BF16)
    keys_t = k_ref[...].astype(F32).T.astype(BF16)
    for b in range(2):
        qg_t = dot(keys_t[:, : SEEN[b]], probs_low[b][...])
        for h in range(HEADS):
            lanes = slice(h * HD, (h + 1) * HD)
            qg_ref[b * RB : (b + 1) * RB, lanes] = qg_t[:, lanes].T.astype(BF16)

    stores[0].start()
    stores[1].start()

    @pl.when(y == w_y)
    def _():
        w_own.wait()

    @pl.when(y != w_y)
    def _():
        remote(wfull.at[w_y, z], wfull.at[w_y, z], w1_send.at[0], w1_recv, y_dev[0]).wait_recv()

    def chunk_part(i, j):
        return wfull.at[w_y, j, :, pl.ds(*WEIGHT_PARTS[i])]

    for i in range(2):
        fan_out(lambda k: chunk_part(i, z), chunk_part(i, z), wz_send.at[i], wz_recv.at[i], z_dev)

    landed(lambda k: parts_in.at[y_from[k]], d1_send, d1_recv, y_dev)
    total_rows = parts_out[y].astype(F32)
    for k in range(NY - 1):
        total_rows = total_rows + parts_in[y_from[k]].astype(F32)
    sums[y] = total_rows[:2].astype(BF16)
    fan_out(lambda k: sums.at[y], sums.at[y], d2_send, d2_recv, y_dev)

    def summed(i):
        return jnp.concatenate([sums[:, i].reshape(NY * ROWS, HD).astype(F32), total_rows[2 + i]], axis=0)

    def block_part(i, block):
        return wfull.at[block, :, :, pl.ds(*WEIGHT_PARTS[i])]

    def send_along_x(i):
        landed(lambda k: chunk_part(i, z_from[k]), wz_send.at[i], wz_recv.at[i], z_dev)
        fan_out(lambda k: block_part(i, w_y), block_part(i, w_y), wx_send.at[i], wx_recv.at[i], x_dev)
        send_core(i, 0, w_y).start()

    def send_core(i, k, block):
        ref = block_part(i, block)
        return remote(ref, ref, wc_send.at[i, k], wc_recv.at[i, k], sibling)

    def forward_to_core(i):
        for k in range(NX - 1):
            ref = block_part(i, 4 * c + x_from[k])
            remote(ref, ref, wx_send.at[i, k], wx_recv.at[i, k], x_dev[k]).wait_recv()
            send_core(i, 1 + k, 4 * c + x_from[k]).start()

    landed(lambda k: sums.at[y_from[k]], d2_send, d2_recv, y_dev)
    fan_out(lambda k: vgfull.at[y], vgfull.at[y], vg_send, vg_recv, y_dev)
    up = summed(1)
    dfg_t = over_tokens(up, x_ref)
    for j in range(NZ - 1):
        rs_src[j] = dfg_t[:, j * 128 : (j + 1) * 128].astype(BF16)
    rs_src[NZ - 1] = over_tokens(summed(0), own_values).astype(BF16)
    fan_out(lambda k: rs_src.at[z_to[k]], rs_dst.at[z], rs_send, rs_recv, z_dev)

    send_along_x(0)

    landed(lambda k: rs_dst.at[z_from[k]], rs_send, rs_recv, z_dev)
    total = rs_src[z].astype(F32)
    for k in range(NZ - 1):
        total = total + rs_dst[z_from[k]].astype(F32)
    bc_buf[x * NC + c] = total.astype(BF16)
    fan_out(lambda k: bc_buf.at[x * NC + c], bc_buf.at[x * NC + c], bc_send, bc_recv, xc_dev)
    send_along_x(1)

    forward_to_core(0)

    landed(lambda k: bc_buf.at[xc_from[k][0] * NC + xc_from[k][1]], bc_send, bc_recv, xc_dev)
    total_ref[...] = sum_of(bc_buf).astype(BF16)
    stores[2].start()
    fan_out(lambda k: total_ref, sums_hbm.at[z], ag_send, ag_recv, z_dev)
    landed(lambda k: vgfull.at[y_from[k]], vg_send, vg_recv, y_dev)
    values = jnp.concatenate([vgfull[j] for j in range(NY)], axis=1)
    up = up.astype(BF16)
    for i in range(2):
        send_core(i, 0, 4 * (1 - c) + x).wait_recv()
        for k in range(NX - 1):
            send_core(i, 1 + k, 4 * (1 - c) + x_from[k]).wait_recv()
        start, size = WEIGHT_PARTS[i]
        for low in range(start, start + size, 256):
            high = min(low + 256, FEATS)
            frozen = dot(values, wfull[:, :, :, low:high].reshape(NY * HD, high - low))
            down = at_ref[:, low:high]
            for rows, factor in ((slice(0, HALF), first(down)), (slice(HALF, CTX), second(down))):
                lig_ref[rows, low:high] = (frozen[rows] + adapter_scale * dot(up, factor)).astype(BF16)
        stores[3 + i].start()
        if i == 0:
            forward_to_core(1)

    landed(lambda k: sums_hbm.at[z_from[k]], ag_send, ag_recv, z_dev)

    for i in range(2):
        send_core(i, 0, w_y).wait_send()
        for k in range(NX - 1):
            send_core(i, 1 + k, 4 * c + x_from[k]).wait_send()
    for copy in pending:
        copy.wait_send()
    for store in stores:
        store.wait()

    @pl.when(y == w_y)
    def _():
        for k in range(NY - 1):
            remote(
                w_hbm.at[w_rows, w_cols(y_to[k])], wfull.at[w_y, z], w1_send.at[k], w1_recv, y_dev[k]
            ).wait_send()


def hand_on(
    lig_hbm, qg_hbm, kg_hbm, sums_hbm,
    lig_out, qg_out, kg_out, dfg_out, ufg_out,
    lig, qg, kg, sums, dfg, ufg, in_sems, out_sems,
):
    pieces = [(sums_hbm, sums, None)]
    for src, via, dst, step in ((lig_hbm, lig, lig_out, 96), (qg_hbm, qg, qg_out, 64), (kg_hbm, kg, kg_out, CTX)):
        for low in range(0, src.shape[0], step):
            rows = pl.ds(low, step)
            pieces.append((src.at[rows], via.at[rows], dst.at[rows]))
    ins = [pltpu.make_async_copy(src, via, in_sems.at[i]) for i, (src, via, _) in enumerate(pieces)]
    outs = [pltpu.make_async_copy(via, dst, out_sems.at[i]) for i, (_, via, dst) in enumerate(pieces[1:])]
    outs += [
        pltpu.make_async_copy(via, dst, out_sems.at[len(outs) + i])
        for i, (via, dst) in enumerate([(dfg, dfg_out), (ufg, ufg_out)])
    ]
    for copy in ins:
        copy.start()
    ins[0].wait()
    for j in range(NZ - 1):
        dfg[:, j * 128 : (j + 1) * 128] = adapter_scale * sums[j].astype(F32)
    ufg[...] = adapter_scale * sums[NZ - 1].astype(F32)
    outs[-2].start()
    outs[-1].start()
    for before, after in zip(ins[1:], outs):
        before.wait()
        after.start()
    for copy in outs:
        copy.wait()


def per_device(
    normed_layer_input,
    queries,
    saved_key_rows,
    saved_value_rows,
    attention_output_gradient,
    finisher_token_mask,
    response_length,
    value_weight_matrix,
    adapter_down_factor,
    adapter_up_factor,
):
    hbm = pl.BlockSpec(memory_space=pltpu.HBM)
    dma = pltpu.SemaphoreType.DMA
    outs = pl.pallas_call(
        kernel,
        out_shape=(
            jax.ShapeDtypeStruct((CTX, FEATS), BF16),
            jax.ShapeDtypeStruct((RESP, FEATS), BF16),
            jax.ShapeDtypeStruct((CTX, HD), BF16),
            jax.ShapeDtypeStruct((NZ, RANK, HD), BF16),
        ),
        in_specs=[hbm] * 10,
        out_specs=(hbm,) * 4,
        scratch_shapes=[
            pltpu.VMEM((CTX, FEATS), BF16),
            pltpu.VMEM((RESP, FEATS), BF16),
            pltpu.VMEM((CTX, HD), BF16),
            pltpu.VMEM((CTX, HD), BF16),
            pltpu.VMEM((RESP, FEATS), BF16),
            pltpu.VMEM((RANK, FEATS), BF16),
            pltpu.VMEM((1, RESP), jnp.int32),
            pltpu.SMEM((1,), jnp.int32),
            pltpu.VMEM((RANK, HD), BF16),
            pltpu.VMEM((NY, NZ, ROWS, FEATS), BF16),
            pltpu.VMEM((NY, CTX, HD), BF16),
            pltpu.VMEM((SEEN[0], FEATS), F32),
            pltpu.VMEM((SEEN[1], FEATS), F32),
            pltpu.VMEM((SEEN[0], FEATS), BF16),
            pltpu.VMEM((SEEN[1], FEATS), BF16),
            pltpu.VMEM((NY, 4, ROWS, HD), BF16),
            pltpu.VMEM((NY, 4, ROWS, HD), BF16),
            pltpu.VMEM((NY, 2, ROWS, HD), BF16),
            pltpu.VMEM((NZ, RANK, HD), BF16),
            pltpu.VMEM((NZ, RANK, HD), BF16),
            pltpu.VMEM((NX * NC, RANK, HD), BF16),
            pltpu.VMEM((RANK, HD), BF16),
            pltpu.VMEM((CTX, FEATS), BF16),
            pltpu.VMEM((RESP, FEATS), BF16),
            pltpu.VMEM((CTX, HD), BF16),
            dma((10,)),
            dma((5,)),
            dma((NY - 1,)),
            dma,
            dma((2, NZ - 1)),
            dma((2, NZ - 1)),
            dma((2, NX - 1)),
            dma((2, NX - 1)),
            dma((2, NX)),
            dma((2, NX)),
            dma((NY - 1,)),
            dma((NY - 1,)),
            dma((NY - 1,)),
            dma((NY - 1,)),
            dma((NY - 1,)),
            dma((NY - 1,)),
            dma((NZ - 1,)),
            dma((NZ - 1,)),
            dma((NX * NC - 1,)),
            dma((NX * NC - 1,)),
            dma((NZ - 1,)),
            dma((NZ - 1,)),
        ],
        compiler_params=pltpu.CompilerParams(
            collective_id=0, has_side_effects=True, vmem_limit_bytes=VMEM_LIMIT
        ),
    )(
        normed_layer_input,
        queries,
        saved_key_rows,
        saved_value_rows,
        attention_output_gradient,
        finisher_token_mask.reshape(1, RESP),
        response_length,
        value_weight_matrix,
        adapter_down_factor.T,
        adapter_up_factor,
    )
    lig, qg, kg, dfg_t, ufg = pl.pallas_call(
        hand_on,
        out_shape=(
            jax.ShapeDtypeStruct((CTX, FEATS), BF16),
            jax.ShapeDtypeStruct((RESP, FEATS), BF16),
            jax.ShapeDtypeStruct((CTX, HD), BF16),
            jax.ShapeDtypeStruct((RANK, FEATS), F32),
            jax.ShapeDtypeStruct((RANK, HD), F32),
        ),
        in_specs=[hbm] * 4,
        out_specs=(hbm,) * 5,
        scratch_shapes=[
            pltpu.VMEM((CTX, FEATS), BF16),
            pltpu.VMEM((RESP, FEATS), BF16),
            pltpu.VMEM((CTX, HD), BF16),
            pltpu.VMEM((NZ, RANK, HD), BF16),
            pltpu.VMEM((RANK, FEATS), F32),
            pltpu.VMEM((RANK, HD), F32),
            dma((9,)),
            dma((10,)),
        ],
        compiler_params=pltpu.CompilerParams(vmem_limit_bytes=VMEM_LIMIT),
    )(*outs)
    return (lig, qg, kg, dfg_t.T, ufg)


def solution(mesh):
    in_specs = (
        P("dp", "tp"),
        P("dp", "tp"),
        P("dp", "tp"),
        P("dp", "tp"),
        P("dp", "tp"),
        P("dp"),
        P("dp"),
        P("tp", None),
        P("tp", None),
        P(None, "tp"),
    )
    out_specs = (P("dp", "tp"), P("dp", "tp"), P("dp", "tp"), P("tp", None), P(None, "tp"))
    return jax.shard_map(
        per_device, mesh=mesh, in_specs=in_specs, out_specs=out_specs, check_vma=False
    )
```

```python
import math

import jax
import jax.numpy as jnp
from jax import lax
from jax.experimental import pallas as pl
from jax.experimental.pallas import tpu as pltpu
from jax.sharding import PartitionSpec as P

MESH = pl.DeviceIdType.MESH
BF16 = jnp.bfloat16
F32 = jnp.float32

QH = 56
KVH = 8
HD = 128
HEADS = QH // KVH
RESP = 256
CTX = 288
PROMPT = CTX - RESP
RANK = 64
FEATS = 896
FACTOR = 1.0 / math.sqrt(HD)
LOG2E = math.log2(math.e)
adapter_scale = 2.0

NX, NZ, NC, NY = 4, 8, 2, 8
HALF = CTX // 2
ROWS = 16

WEIGHT_PARTS = ((0, 512), (512, 384))

FAR_FIRST = (4, 3, 5, 2, 6, 1, 7)

RB = 128
SEEN = (PROMPT + RB, CTX)

VMEM_LIMIT = 60 * 1024 * 1024

NT = (((1,), (1,)), ((), ()))


def dot(a, b):
    return jnp.dot(a, b, preferred_element_type=F32)


def dot_nt(a, b):
    return lax.dot_general(a, b, NT, preferred_element_type=F32)


def rows_of_heads(ref, b):
    return jnp.concatenate(
        [ref[b * RB : (b + 1) * RB, h * HD : (h + 1) * HD] for h in range(HEADS)], axis=0
    )


def kernel(
    x_hbm, q_hbm, k_hbm, v_hbm, g_hbm, mask_hbm, length_hbm, w_hbm, at_hbm, b_hbm,
    lig_hbm, qg_hbm, kg_hbm, sums_hbm,
    x_ref, q_ref, k_ref, v_ref, g_ref, at_ref, mask_ref, length_ref,
    b_ref, wfull, vgfull,
    p0, p1, pb0, pb1,
    parts_out, parts_in, sums,
    rs_src, rs_dst, bc_buf, total_ref,
    lig_ref, qg_ref, kg_ref,
    load_sem, store_sem, w1_send, w1_recv, wz_send, wz_recv, wx_send, wx_recv, wc_send, wc_recv,
    d1_send, d1_recv, d2_send, d2_recv, vg_send, vg_recv,
    rs_send, rs_recv, bc_send, bc_recv, ag_send, ag_recv,
):
    dp = lax.axis_index("dp")
    y = lax.axis_index("tp")
    x = dp // (NZ * NC)
    z = (dp // NC) % NZ
    c = dp % NC

    def at(px, pz, pc, py):
        return {"dp": (px * NZ + pz) * NC + pc, "tp": py}

    y_to = [(y + k) % NY for k in FAR_FIRST]
    y_from = [(y + NY - k) % NY for k in FAR_FIRST]
    z_to = [(z + k) % NZ for k in FAR_FIRST]
    z_from = [(z + NZ - k) % NZ for k in FAR_FIRST]
    x_to = [(x + k) % NX for k in (2, 1, 3)]
    x_from = [(x + NX - k) % NX for k in (2, 1, 3)]
    xc_steps = [(i, j) for i in (2, 1, 3, 0) for j in (1, 0) if i or j]
    xc_to = [((x + i) % NX, (c + j) % NC) for i, j in xc_steps]
    xc_from = [((x + NX - i) % NX, (c + NC - j) % NC) for i, j in xc_steps]
    y_dev = [at(x, z, c, j) for j in y_to]
    z_dev = [at(x, j, c, y) for j in z_to]
    x_dev = [at(j, z, c, y) for j in x_to]
    xc_dev = [at(i, z, j, y) for i, j in xc_to]
    sibling = at(x, z, 1 - c, y)

    def remote(src, dst, send, recv, device):
        return pltpu.make_async_remote_copy(
            src_ref=src, dst_ref=dst, send_sem=send, recv_sem=recv, device_id=device, device_id_type=MESH
        )

    pending = []
    stores = [
        pltpu.make_async_copy(src, dst, store_sem.at[i])
        for i, (src, dst) in enumerate(
            [(qg_ref, qg_hbm), (kg_ref, kg_hbm), (total_ref, sums_hbm.at[z])]
            + [(lig_ref.at[:, pl.ds(*cols)], lig_hbm.at[:, pl.ds(*cols)]) for cols in WEIGHT_PARTS]
        )
    ]

    def fan_out(src, dst, send, recv, devices):
        for k, device in enumerate(devices):
            copy = remote(src(k), dst, send.at[k], recv.at[k], device)
            copy.start()
            pending.append(copy)

    def landed(dst, send, recv, devices):
        for k, device in enumerate(devices):
            remote(dst(k), dst(k), send.at[k], recv.at[k], device).wait_recv()

    w_y = 4 * c + x
    w_rows = pl.ds(pl.multiple_of(z * ROWS, ROWS), ROWS)

    def w_cols(j):
        return pl.ds(pl.multiple_of(j * FEATS, 128), FEATS)

    loads = [
        pltpu.make_async_copy(src, dst, load_sem.at[i])
        for i, (src, dst) in enumerate(
            [
                (k_hbm, k_ref),
                (q_hbm, q_ref),
                (x_hbm, x_ref),
                (at_hbm, at_ref),
                (g_hbm, g_ref),
                (v_hbm, v_ref),
                (b_hbm, b_ref),
                (mask_hbm, mask_ref),
                (length_hbm, length_ref),
            ]
        )
    ]
    for load in loads:
        load.start()
    barrier = pltpu.get_barrier_semaphore()
    everyone = y_dev + z_dev + xc_dev
    for device in everyone:
        pl.semaphore_signal(barrier, inc=1, device_id=device, device_id_type=MESH)

    load_k, load_q, load_x, load_a, load_g, load_v, load_b, load_mask, load_length = loads
    w_own = pltpu.make_async_copy(w_hbm.at[w_rows, w_cols(y)], wfull.at[w_y, z], load_sem.at[9])

    @pl.when(y == w_y)
    def _():
        w_own.start()

    def first(factor):
        return jnp.concatenate([factor, jnp.zeros_like(factor)], axis=0)

    def second(factor):
        return jnp.concatenate([jnp.zeros_like(factor), factor], axis=0)

    def rank_rows(rows, factor):
        return dot_nt(rows[:HALF], first(factor)) + dot_nt(rows[HALF:], second(factor))

    def over_tokens(pairs, rows):
        pairs_t = pairs.T.astype(BF16)
        return dot(pairs_t, rows[:HALF])[:RANK] + dot(pairs_t, rows[HALF:])[RANK:]

    def sum_of(parts):
        total = parts[0].astype(F32)
        for j in range(1, parts.shape[0]):
            total = total + parts[j].astype(F32)
        return total

    for load in (load_k, load_q, load_mask, load_length, load_x, load_a, load_g, load_b):
        load.wait()
    limit = PROMPT - 1 + length_ref[0]
    probs = (p0, p1)
    probs_low = (pb0, pb1)

    def weigh(b, h):
        seen = SEEN[b]
        q = q_ref[b * RB : (b + 1) * RB, h * HD : (h + 1) * HD]
        scores = dot_nt(k_ref[:seen, :], q) * (FACTOR * LOG2E)
        col = lax.broadcasted_iota(jnp.int32, (seen, RB), 0)
        row = lax.broadcasted_iota(jnp.int32, (1, RB), 1) + b * RB
        last = jnp.minimum(row + PROMPT, limit)
        scores = jnp.where(col <= last, scores, -1e30)
        top = jnp.max(scores, axis=0, keepdims=True)
        expo = jnp.exp2(scores - top)
        keep = jnp.where(row + PROMPT <= limit, mask_ref[:, b * RB : (b + 1) * RB], 0).astype(F32)
        p = expo * (keep / jnp.sum(expo, axis=0, keepdims=True))
        probs[b][:, h * HD : (h + 1) * HD] = p
        probs_low[b][:, h * HD : (h + 1) * HD] = p.astype(BF16)

    for h in range(HEADS):
        for b in range(2):
            weigh(b, h)

    def hand_out(i, rows):
        rows = rows.astype(BF16)
        for j in range(NY):
            parts_out[j, i] = rows[j * ROWS : (j + 1) * ROWS]
            parts_out[j, 2 + i] = rows[NY * ROWS :]

    hand_out(0, rank_rows(x_ref, at_ref[...]))
    early = dot(pb0[...], rows_of_heads(g_ref, 0))
    late = dot(pb1[...], rows_of_heads(g_ref, 1))
    vgfull[y, : SEEN[0], :] = (early + late[: SEEN[0]]).astype(BF16)
    vgfull[y, SEEN[0] :, :] = late[SEEN[0] :].astype(BF16)
    own_values = vgfull[y]
    hand_out(1, rank_rows(own_values, b_ref[...]))

    pl.semaphore_wait(barrier, len(everyone))

    fan_out(lambda k: parts_out.at[y_to[k]], parts_in.at[y], d1_send, d1_recv, y_dev)

    @pl.when(y == w_y)
    def _():
        for k in range(NY - 1):
            remote(
                w_hbm.at[w_rows, w_cols(y_to[k])], wfull.at[w_y, z], w1_send.at[k], w1_recv, y_dev[k]
            ).start()

    landed(lambda k: parts_in.at[y_from[k]], d1_send, d1_recv, y_dev)
    total_rows = parts_out[y].astype(F32)
    for k in range(NY - 1):
        total_rows = total_rows + parts_in[y_from[k]].astype(F32)
    sums[y] = total_rows[:2].astype(BF16)
    fan_out(lambda k: sums.at[y], sums.at[y], d2_send, d2_recv, y_dev)

    @pl.when(y == w_y)
    def _():
        w_own.wait()

    @pl.when(y != w_y)
    def _():
        remote(wfull.at[w_y, z], wfull.at[w_y, z], w1_send.at[0], w1_recv, y_dev[0]).wait_recv()

    def chunk_part(i, j):
        return wfull.at[w_y, j, :, pl.ds(*WEIGHT_PARTS[i])]

    for i in range(2):
        fan_out(lambda k: chunk_part(i, z), chunk_part(i, z), wz_send.at[i], wz_recv.at[i], z_dev)

    load_v.wait()
    for h in range(HEADS):
        for b in range(2):
            seen = SEEN[b]
            lanes = slice(h * HD, (h + 1) * HD)
            p = probs[b][:, lanes]
            t = p * dot_nt(v_ref[:seen, :], g_ref[b * RB : (b + 1) * RB, lanes])
            probs_low[b][:, lanes] = ((t - p * jnp.sum(t, axis=0, keepdims=True)) * FACTOR).astype(BF16)

    early = dot(pb0[...], rows_of_heads(q_ref, 0))
    late = dot(pb1[...], rows_of_heads(q_ref, 1))
    kg_ref[: SEEN[0], :] = (early + late[: SEEN[0]]).astype(BF16)
    kg_ref[SEEN[0] :, :] = late[SEEN[0] :].astype(BF16)
    keys_t = k_ref[...].astype(F32).T.astype(BF16)
    for b in range(2):
        qg_t = dot(keys_t[:, : SEEN[b]], probs_low[b][...])
        for h in range(HEADS):
            lanes = slice(h * HD, (h + 1) * HD)
            qg_ref[b * RB : (b + 1) * RB, lanes] = qg_t[:, lanes].T.astype(BF16)

    stores[0].start()
    stores[1].start()

    def summed(i):
        return jnp.concatenate([sums[:, i].reshape(NY * ROWS, HD).astype(F32), total_rows[2 + i]], axis=0)

    def block_part(i, block):
        return wfull.at[block, :, :, pl.ds(*WEIGHT_PARTS[i])]

    def send_along_x(i):
        landed(lambda k: chunk_part(i, z_from[k]), wz_send.at[i], wz_recv.at[i], z_dev)
        fan_out(lambda k: block_part(i, w_y), block_part(i, w_y), wx_send.at[i], wx_recv.at[i], x_dev)
        send_core(i, 0, w_y).start()

    def send_core(i, k, block):
        ref = block_part(i, block)
        return remote(ref, ref, wc_send.at[i, k], wc_recv.at[i, k], sibling)

    def forward_to_core(i):
        for k in range(NX - 1):
            ref = block_part(i, 4 * c + x_from[k])
            remote(ref, ref, wx_send.at[i, k], wx_recv.at[i, k], x_dev[k]).wait_recv()
            send_core(i, 1 + k, 4 * c + x_from[k]).start()

    landed(lambda k: sums.at[y_from[k]], d2_send, d2_recv, y_dev)
    fan_out(lambda k: vgfull.at[y], vgfull.at[y], vg_send, vg_recv, y_dev)
    up = summed(1)
    dfg_t = over_tokens(up, x_ref)
    for j in range(NZ - 1):
        rs_src[j] = dfg_t[:, j * 128 : (j + 1) * 128].astype(BF16)
    rs_src[NZ - 1] = over_tokens(summed(0), own_values).astype(BF16)
    fan_out(lambda k: rs_src.at[z_to[k]], rs_dst.at[z], rs_send, rs_recv, z_dev)

    send_along_x(0)

    landed(lambda k: rs_dst.at[z_from[k]], rs_send, rs_recv, z_dev)
    total = rs_src[z].astype(F32)
    for k in range(NZ - 1):
        total = total + rs_dst[z_from[k]].astype(F32)
    bc_buf[x * NC + c] = total.astype(BF16)
    fan_out(lambda k: bc_buf.at[x * NC + c], bc_buf.at[x * NC + c], bc_send, bc_recv, xc_dev)
    send_along_x(1)

    forward_to_core(0)

    landed(lambda k: bc_buf.at[xc_from[k][0] * NC + xc_from[k][1]], bc_send, bc_recv, xc_dev)
    total_ref[...] = sum_of(bc_buf).astype(BF16)
    stores[2].start()
    fan_out(lambda k: total_ref, sums_hbm.at[z], ag_send, ag_recv, z_dev)
    landed(lambda k: vgfull.at[y_from[k]], vg_send, vg_recv, y_dev)
    values = jnp.concatenate([vgfull[j] for j in range(NY)], axis=1)
    up = up.astype(BF16)
    for i in range(2):
        send_core(i, 0, 4 * (1 - c) + x).wait_recv()
        for k in range(NX - 1):
            send_core(i, 1 + k, 4 * (1 - c) + x_from[k]).wait_recv()
        start, size = WEIGHT_PARTS[i]
        for low in range(start, start + size, 256):
            high = min(low + 256, FEATS)
            frozen = dot(values, wfull[:, :, :, low:high].reshape(NY * HD, high - low))
            down = at_ref[:, low:high]
            for rows, factor in ((slice(0, HALF), first(down)), (slice(HALF, CTX), second(down))):
                lig_ref[rows, low:high] = (frozen[rows] + adapter_scale * dot(up, factor)).astype(BF16)
        stores[3 + i].start()
        if i == 0:
            forward_to_core(1)

    landed(lambda k: sums_hbm.at[z_from[k]], ag_send, ag_recv, z_dev)

    for i in range(2):
        send_core(i, 0, w_y).wait_send()
        for k in range(NX - 1):
            send_core(i, 1 + k, 4 * c + x_from[k]).wait_send()
    for copy in pending:
        copy.wait_send()
    for store in stores:
        store.wait()

    @pl.when(y == w_y)
    def _():
        for k in range(NY - 1):
            remote(
                w_hbm.at[w_rows, w_cols(y_to[k])], wfull.at[w_y, z], w1_send.at[k], w1_recv, y_dev[k]
            ).wait_send()


def hand_on(
    lig_hbm, qg_hbm, kg_hbm, sums_hbm,
    lig_out, qg_out, kg_out, dfg_out, ufg_out,
    lig, qg, kg, sums, dfg, ufg, in_sems, out_sems,
):
    pieces = [(sums_hbm, sums, None)]
    for src, via, dst, step in ((lig_hbm, lig, lig_out, 96), (qg_hbm, qg, qg_out, 64), (kg_hbm, kg, kg_out, CTX)):
        for low in range(0, src.shape[0], step):
            rows = pl.ds(low, step)
            pieces.append((src.at[rows], via.at[rows], dst.at[rows]))
    ins = [pltpu.make_async_copy(src, via, in_sems.at[i]) for i, (src, via, _) in enumerate(pieces)]
    outs = [pltpu.make_async_copy(via, dst, out_sems.at[i]) for i, (_, via, dst) in enumerate(pieces[1:])]
    outs += [
        pltpu.make_async_copy(via, dst, out_sems.at[len(outs) + i])
        for i, (via, dst) in enumerate([(dfg, dfg_out), (ufg, ufg_out)])
    ]
    for copy in ins:
        copy.start()
    ins[0].wait()
    for j in range(NZ - 1):
        dfg[:, j * 128 : (j + 1) * 128] = adapter_scale * sums[j].astype(F32)
    ufg[...] = adapter_scale * sums[NZ - 1].astype(F32)
    outs[-2].start()
    outs[-1].start()
    for before, after in zip(ins[1:], outs):
        before.wait()
        after.start()
    for copy in outs:
        copy.wait()


def per_device(
    normed_layer_input,
    queries,
    saved_key_rows,
    saved_value_rows,
    attention_output_gradient,
    finisher_token_mask,
    response_length,
    value_weight_matrix,
    adapter_down_factor,
    adapter_up_factor,
):
    hbm = pl.BlockSpec(memory_space=pltpu.HBM)
    dma = pltpu.SemaphoreType.DMA
    outs = pl.pallas_call(
        kernel,
        out_shape=(
            jax.ShapeDtypeStruct((CTX, FEATS), BF16),
            jax.ShapeDtypeStruct((RESP, FEATS), BF16),
            jax.ShapeDtypeStruct((CTX, HD), BF16),
            jax.ShapeDtypeStruct((NZ, RANK, HD), BF16),
        ),
        in_specs=[hbm] * 10,
        out_specs=(hbm,) * 4,
        scratch_shapes=[
            pltpu.VMEM((CTX, FEATS), BF16),
            pltpu.VMEM((RESP, FEATS), BF16),
            pltpu.VMEM((CTX, HD), BF16),
            pltpu.VMEM((CTX, HD), BF16),
            pltpu.VMEM((RESP, FEATS), BF16),
            pltpu.VMEM((RANK, FEATS), BF16),
            pltpu.VMEM((1, RESP), jnp.int32),
            pltpu.SMEM((1,), jnp.int32),
            pltpu.VMEM((RANK, HD), BF16),
            pltpu.VMEM((NY, NZ, ROWS, FEATS), BF16),
            pltpu.VMEM((NY, CTX, HD), BF16),
            pltpu.VMEM((SEEN[0], FEATS), F32),
            pltpu.VMEM((SEEN[1], FEATS), F32),
            pltpu.VMEM((SEEN[0], FEATS), BF16),
            pltpu.VMEM((SEEN[1], FEATS), BF16),
            pltpu.VMEM((NY, 4, ROWS, HD), BF16),
            pltpu.VMEM((NY, 4, ROWS, HD), BF16),
            pltpu.VMEM((NY, 2, ROWS, HD), BF16),
            pltpu.VMEM((NZ, RANK, HD), BF16),
            pltpu.VMEM((NZ, RANK, HD), BF16),
            pltpu.VMEM((NX * NC, RANK, HD), BF16),
            pltpu.VMEM((RANK, HD), BF16),
            pltpu.VMEM((CTX, FEATS), BF16),
            pltpu.VMEM((RESP, FEATS), BF16),
            pltpu.VMEM((CTX, HD), BF16),
            dma((10,)),
            dma((5,)),
            dma((NY - 1,)),
            dma,
            dma((2, NZ - 1)),
            dma((2, NZ - 1)),
            dma((2, NX - 1)),
            dma((2, NX - 1)),
            dma((2, NX)),
            dma((2, NX)),
            dma((NY - 1,)),
            dma((NY - 1,)),
            dma((NY - 1,)),
            dma((NY - 1,)),
            dma((NY - 1,)),
            dma((NY - 1,)),
            dma((NZ - 1,)),
            dma((NZ - 1,)),
            dma((NX * NC - 1,)),
            dma((NX * NC - 1,)),
            dma((NZ - 1,)),
            dma((NZ - 1,)),
        ],
        compiler_params=pltpu.CompilerParams(
            collective_id=0, has_side_effects=True, vmem_limit_bytes=VMEM_LIMIT
        ),
    )(
        normed_layer_input,
        queries,
        saved_key_rows,
        saved_value_rows,
        attention_output_gradient,
        finisher_token_mask.reshape(1, RESP),
        response_length,
        value_weight_matrix,
        adapter_down_factor.T,
        adapter_up_factor,
    )
    lig, qg, kg, dfg_t, ufg = pl.pallas_call(
        hand_on,
        out_shape=(
            jax.ShapeDtypeStruct((CTX, FEATS), BF16),
            jax.ShapeDtypeStruct((RESP, FEATS), BF16),
            jax.ShapeDtypeStruct((CTX, HD), BF16),
            jax.ShapeDtypeStruct((RANK, FEATS), F32),
            jax.ShapeDtypeStruct((RANK, HD), F32),
        ),
        in_specs=[hbm] * 4,
        out_specs=(hbm,) * 5,
        scratch_shapes=[
            pltpu.VMEM((CTX, FEATS), BF16),
            pltpu.VMEM((RESP, FEATS), BF16),
            pltpu.VMEM((CTX, HD), BF16),
            pltpu.VMEM((NZ, RANK, HD), BF16),
            pltpu.VMEM((RANK, FEATS), F32),
            pltpu.VMEM((RANK, HD), F32),
            dma((9,)),
            dma((10,)),
        ],
        compiler_params=pltpu.CompilerParams(vmem_limit_bytes=VMEM_LIMIT),
    )(*outs)
    return (lig, qg, kg, dfg_t.T, ufg)


def solution(mesh):
    in_specs = (
        P("dp", "tp"),
        P("dp", "tp"),
        P("dp", "tp"),
        P("dp", "tp"),
        P("dp", "tp"),
        P("dp"),
        P("dp"),
        P("tp", None),
        P("tp", None),
        P(None, "tp"),
    )
    out_specs = (P("dp", "tp"), P("dp", "tp"), P("dp", "tp"), P("tp", None), P(None, "tp"))
    return jax.shard_map(
        per_device, mesh=mesh, in_specs=in_specs, out_specs=out_specs, check_vma=False
    )
```

```python
import math

import jax
import jax.numpy as jnp
from jax import lax
from jax.experimental import pallas as pl
from jax.experimental.pallas import tpu as pltpu
from jax.sharding import PartitionSpec as P

MESH = pl.DeviceIdType.MESH
BF16 = jnp.bfloat16
F32 = jnp.float32

QH = 56
KVH = 8
HD = 128
HEADS = QH // KVH
RESP = 256
CTX = 288
PROMPT = CTX - RESP
RANK = 64
FEATS = 896
FACTOR = 1.0 / math.sqrt(HD)
LOG2E = math.log2(math.e)
adapter_scale = 2.0

NX, NZ, NC, NY = 4, 8, 2, 8
HALF = CTX // 2
ROWS = 16

WEIGHT_PARTS = ((0, 512), (512, 384))

FAR_FIRST = (4, 3, 5, 2, 6, 1, 7)

RB = 128
SEEN = (PROMPT + RB, CTX)

VMEM_LIMIT = 60 * 1024 * 1024

NT = (((1,), (1,)), ((), ()))


def dot(a, b):
    return jnp.dot(a, b, preferred_element_type=F32)


def dot_nt(a, b):
    return lax.dot_general(a, b, NT, preferred_element_type=F32)


def rows_of_heads(ref, b):
    return jnp.concatenate(
        [ref[b * RB : (b + 1) * RB, h * HD : (h + 1) * HD] for h in range(HEADS)], axis=0
    )


def kernel(
    x_hbm, q_hbm, k_hbm, v_hbm, g_hbm, mask_hbm, length_hbm, w_hbm, at_hbm, b_hbm,
    lig_hbm, qg_hbm, kg_hbm, sums_hbm,
    x_ref, q_ref, k_ref, v_ref, g_ref, at_ref, mask_ref, length_ref,
    b_ref, wfull, vgfull,
    p0, p1, pb0, pb1,
    parts_out, parts_in, sums,
    rs_src, rs_dst, bc_buf, total_ref,
    lig_ref, qg_ref, kg_ref,
    load_sem, store_sem, w1_send, w1_recv, wz_send, wz_recv, wx_send, wx_recv, wc_send, wc_recv,
    d1_send, d1_recv, d2_send, d2_recv, vg_send, vg_recv,
    rs_send, rs_recv, bc_send, bc_recv, ag_send, ag_recv,
):
    dp = lax.axis_index("dp")
    y = lax.axis_index("tp")
    x = dp // (NZ * NC)
    z = (dp // NC) % NZ
    c = dp % NC

    def at(px, pz, pc, py):
        return {"dp": (px * NZ + pz) * NC + pc, "tp": py}

    y_to = [(y + k) % NY for k in FAR_FIRST]
    y_from = [(y + NY - k) % NY for k in FAR_FIRST]
    z_to = [(z + k) % NZ for k in FAR_FIRST]
    z_from = [(z + NZ - k) % NZ for k in FAR_FIRST]
    x_to = [(x + k) % NX for k in (2, 1, 3)]
    x_from = [(x + NX - k) % NX for k in (2, 1, 3)]
    xc_steps = [(i, j) for i in (2, 1, 3, 0) for j in (1, 0) if i or j]
    xc_to = [((x + i) % NX, (c + j) % NC) for i, j in xc_steps]
    xc_from = [((x + NX - i) % NX, (c + NC - j) % NC) for i, j in xc_steps]
    y_dev = [at(x, z, c, j) for j in y_to]
    z_dev = [at(x, j, c, y) for j in z_to]
    x_dev = [at(j, z, c, y) for j in x_to]
    xc_dev = [at(i, z, j, y) for i, j in xc_to]
    sibling = at(x, z, 1 - c, y)

    def remote(src, dst, send, recv, device):
        return pltpu.make_async_remote_copy(
            src_ref=src, dst_ref=dst, send_sem=send, recv_sem=recv, device_id=device, device_id_type=MESH
        )

    pending = []
    stores = [
        pltpu.make_async_copy(src, dst, store_sem.at[i])
        for i, (src, dst) in enumerate(
            [(qg_ref, qg_hbm), (kg_ref, kg_hbm), (total_ref, sums_hbm.at[z])]
            + [(lig_ref.at[:, pl.ds(*cols)], lig_hbm.at[:, pl.ds(*cols)]) for cols in WEIGHT_PARTS]
        )
    ]

    def fan_out(src, dst, send, recv, devices):
        for k, device in enumerate(devices):
            copy = remote(src(k), dst, send.at[k], recv.at[k], device)
            copy.start()
            pending.append(copy)

    def landed(dst, send, recv, devices):
        for k, device in enumerate(devices):
            remote(dst(k), dst(k), send.at[k], recv.at[k], device).wait_recv()

    w_y = 4 * c + x
    w_rows = pl.ds(pl.multiple_of(z * ROWS, ROWS), ROWS)

    def w_cols(j):
        return pl.ds(pl.multiple_of(j * FEATS, 128), FEATS)

    loads = [
        pltpu.make_async_copy(src, dst, load_sem.at[i])
        for i, (src, dst) in enumerate(
            [
                (k_hbm, k_ref),
                (q_hbm, q_ref),
                (x_hbm, x_ref),
                (at_hbm, at_ref),
                (g_hbm, g_ref),
                (v_hbm, v_ref),
                (b_hbm, b_ref),
                (mask_hbm, mask_ref),
                (length_hbm, length_ref),
            ]
        )
    ]
    for load in loads:
        load.start()
    barrier = pltpu.get_barrier_semaphore()
    everyone = y_dev + z_dev + xc_dev
    for device in everyone:
        pl.semaphore_signal(barrier, inc=1, device_id=device, device_id_type=MESH)

    load_k, load_q, load_x, load_a, load_g, load_v, load_b, load_mask, load_length = loads
    w_own = pltpu.make_async_copy(w_hbm.at[w_rows, w_cols(y)], wfull.at[w_y, z], load_sem.at[9])

    @pl.when(y == w_y)
    def _():
        w_own.start()

    def first(factor):
        return jnp.concatenate([factor, jnp.zeros_like(factor)], axis=0)

    def second(factor):
        return jnp.concatenate([jnp.zeros_like(factor), factor], axis=0)

    def rank_rows(rows, factor):
        return dot_nt(rows[:HALF], first(factor)) + dot_nt(rows[HALF:], second(factor))

    def over_tokens(pairs, rows):
        pairs_t = pairs.T.astype(BF16)
        return dot(pairs_t, rows[:HALF])[:RANK] + dot(pairs_t, rows[HALF:])[RANK:]

    def sum_of(parts):
        total = parts[0].astype(F32)
        for j in range(1, parts.shape[0]):
            total = total + parts[j].astype(F32)
        return total

    for load in (load_k, load_q, load_mask, load_length, load_x, load_a, load_g, load_b):
        load.wait()
    limit = PROMPT - 1 + length_ref[0]
    probs = (p0, p1)
    probs_low = (pb0, pb1)

    def weigh(b, h):
        seen = SEEN[b]
        q = q_ref[b * RB : (b + 1) * RB, h * HD : (h + 1) * HD]
        scores = dot_nt(k_ref[:seen, :], q) * (FACTOR * LOG2E)
        col = lax.broadcasted_iota(jnp.int32, (seen, RB), 0)
        row = lax.broadcasted_iota(jnp.int32, (1, RB), 1) + b * RB
        last = jnp.minimum(row + PROMPT, limit)
        scores = jnp.where(col <= last, scores, -1e30)
        top = jnp.max(scores, axis=0, keepdims=True)
        expo = jnp.exp2(scores - top)
        keep = jnp.where(row + PROMPT <= limit, mask_ref[:, b * RB : (b + 1) * RB], 0).astype(F32)
        p = expo * (keep / jnp.sum(expo, axis=0, keepdims=True))
        probs[b][:, h * HD : (h + 1) * HD] = p
        probs_low[b][:, h * HD : (h + 1) * HD] = p.astype(BF16)

    for h in range(HEADS):
        for b in range(2):
            weigh(b, h)

    def hand_out(i, rows):
        rows = rows.astype(BF16)
        for j in range(NY):
            parts_out[j, i] = rows[j * ROWS : (j + 1) * ROWS]
            parts_out[j, 2 + i] = rows[NY * ROWS :]

    hand_out(0, rank_rows(x_ref, at_ref[...]))
    early = dot(pb0[...], rows_of_heads(g_ref, 0))
    late = dot(pb1[...], rows_of_heads(g_ref, 1))
    vgfull[y, : SEEN[0], :] = (early + late[: SEEN[0]]).astype(BF16)
    vgfull[y, SEEN[0] :, :] = late[SEEN[0] :].astype(BF16)
    own_values = vgfull[y]
    hand_out(1, rank_rows(own_values, b_ref[...]))

    pl.semaphore_wait(barrier, len(everyone))

    fan_out(lambda k: parts_out.at[y_to[k]], parts_in.at[y], d1_send, d1_recv, y_dev)

    @pl.when(y == w_y)
    def _():
        for k in range(NY - 1):
            remote(
                w_hbm.at[w_rows, w_cols(y_to[k])], wfull.at[w_y, z], w1_send.at[k], w1_recv, y_dev[k]
            ).start()

    landed(lambda k: parts_in.at[y_from[k]], d1_send, d1_recv, y_dev)
    total_rows = parts_out[y].astype(F32)
    for k in range(NY - 1):
        total_rows = total_rows + parts_in[y_from[k]].astype(F32)
    sums[y] = total_rows[:2].astype(BF16)
    fan_out(lambda k: sums.at[y], sums.at[y], d2_send, d2_recv, y_dev)

    @pl.when(y == w_y)
    def _():
        w_own.wait()

    @pl.when(y != w_y)
    def _():
        remote(wfull.at[w_y, z], wfull.at[w_y, z], w1_send.at[0], w1_recv, y_dev[0]).wait_recv()

    def chunk_part(i, j):
        return wfull.at[w_y, j, :, pl.ds(*WEIGHT_PARTS[i])]

    for i in range(2):
        fan_out(lambda k: chunk_part(i, z), chunk_part(i, z), wz_send.at[i], wz_recv.at[i], z_dev)

    def summed(i):
        return jnp.concatenate([sums[:, i].reshape(NY * ROWS, HD).astype(F32), total_rows[2 + i]], axis=0)

    def block_part(i, block):
        return wfull.at[block, :, :, pl.ds(*WEIGHT_PARTS[i])]

    def send_along_x(i):
        landed(lambda k: chunk_part(i, z_from[k]), wz_send.at[i], wz_recv.at[i], z_dev)
        fan_out(lambda k: block_part(i, w_y), block_part(i, w_y), wx_send.at[i], wx_recv.at[i], x_dev)
        send_core(i, 0, w_y).start()

    def send_core(i, k, block):
        ref = block_part(i, block)
        return remote(ref, ref, wc_send.at[i, k], wc_recv.at[i, k], sibling)

    def forward_to_core(i):
        for k in range(NX - 1):
            ref = block_part(i, 4 * c + x_from[k])
            remote(ref, ref, wx_send.at[i, k], wx_recv.at[i, k], x_dev[k]).wait_recv()
            send_core(i, 1 + k, 4 * c + x_from[k]).start()

    landed(lambda k: sums.at[y_from[k]], d2_send, d2_recv, y_dev)
    up = summed(1)
    dfg_t = over_tokens(up, x_ref)
    for j in range(NZ - 1):
        rs_src[j] = dfg_t[:, j * 128 : (j + 1) * 128].astype(BF16)
    rs_src[NZ - 1] = over_tokens(summed(0), own_values).astype(BF16)
    fan_out(lambda k: rs_src.at[z_to[k]], rs_dst.at[z], rs_send, rs_recv, z_dev)
    fan_out(lambda k: vgfull.at[y], vgfull.at[y], vg_send, vg_recv, y_dev)

    load_v.wait()
    for h in range(HEADS):
        for b in range(2):
            seen = SEEN[b]
            lanes = slice(h * HD, (h + 1) * HD)
            p = probs[b][:, lanes]
            t = p * dot_nt(v_ref[:seen, :], g_ref[b * RB : (b + 1) * RB, lanes])
            probs_low[b][:, lanes] = ((t - p * jnp.sum(t, axis=0, keepdims=True)) * FACTOR).astype(BF16)

    early = dot(pb0[...], rows_of_heads(q_ref, 0))
    late = dot(pb1[...], rows_of_heads(q_ref, 1))
    kg_ref[: SEEN[0], :] = (early + late[: SEEN[0]]).astype(BF16)
    kg_ref[SEEN[0] :, :] = late[SEEN[0] :].astype(BF16)
    keys_t = k_ref[...].astype(F32).T.astype(BF16)
    for b in range(2):
        qg_t = dot(keys_t[:, : SEEN[b]], probs_low[b][...])
        for h in range(HEADS):
            lanes = slice(h * HD, (h + 1) * HD)
            qg_ref[b * RB : (b + 1) * RB, lanes] = qg_t[:, lanes].T.astype(BF16)

    stores[0].start()
    stores[1].start()

    send_along_x(0)

    landed(lambda k: rs_dst.at[z_from[k]], rs_send, rs_recv, z_dev)
    total = rs_src[z].astype(F32)
    for k in range(NZ - 1):
        total = total + rs_dst[z_from[k]].astype(F32)
    bc_buf[x * NC + c] = total.astype(BF16)
    fan_out(lambda k: bc_buf.at[x * NC + c], bc_buf.at[x * NC + c], bc_send, bc_recv, xc_dev)
    send_along_x(1)

    forward_to_core(0)

    landed(lambda k: bc_buf.at[xc_from[k][0] * NC + xc_from[k][1]], bc_send, bc_recv, xc_dev)
    total_ref[...] = sum_of(bc_buf).astype(BF16)
    stores[2].start()
    fan_out(lambda k: total_ref, sums_hbm.at[z], ag_send, ag_recv, z_dev)
    landed(lambda k: vgfull.at[y_from[k]], vg_send, vg_recv, y_dev)
    values = jnp.concatenate([vgfull[j] for j in range(NY)], axis=1)
    up = up.astype(BF16)
    for i in range(2):
        send_core(i, 0, 4 * (1 - c) + x).wait_recv()
        for k in range(NX - 1):
            send_core(i, 1 + k, 4 * (1 - c) + x_from[k]).wait_recv()
        start, size = WEIGHT_PARTS[i]
        for low in range(start, start + size, 256):
            high = min(low + 256, FEATS)
            frozen = dot(values, wfull[:, :, :, low:high].reshape(NY * HD, high - low))
            down = at_ref[:, low:high]
            for rows, factor in ((slice(0, HALF), first(down)), (slice(HALF, CTX), second(down))):
                lig_ref[rows, low:high] = (frozen[rows] + adapter_scale * dot(up, factor)).astype(BF16)
        stores[3 + i].start()
        if i == 0:
            forward_to_core(1)

    landed(lambda k: sums_hbm.at[z_from[k]], ag_send, ag_recv, z_dev)

    for i in range(2):
        send_core(i, 0, w_y).wait_send()
        for k in range(NX - 1):
            send_core(i, 1 + k, 4 * c + x_from[k]).wait_send()
    for copy in pending:
        copy.wait_send()
    for store in stores:
        store.wait()

    @pl.when(y == w_y)
    def _():
        for k in range(NY - 1):
            remote(
                w_hbm.at[w_rows, w_cols(y_to[k])], wfull.at[w_y, z], w1_send.at[k], w1_recv, y_dev[k]
            ).wait_send()


def hand_on(
    lig_hbm, qg_hbm, kg_hbm, sums_hbm,
    lig_out, qg_out, kg_out, dfg_out, ufg_out,
    lig, qg, kg, sums, dfg, ufg, in_sems, out_sems,
):
    pieces = [(sums_hbm, sums, None)]
    for src, via, dst, step in ((lig_hbm, lig, lig_out, 96), (qg_hbm, qg, qg_out, 64), (kg_hbm, kg, kg_out, CTX)):
        for low in range(0, src.shape[0], step):
            rows = pl.ds(low, step)
            pieces.append((src.at[rows], via.at[rows], dst.at[rows]))
    ins = [pltpu.make_async_copy(src, via, in_sems.at[i]) for i, (src, via, _) in enumerate(pieces)]
    outs = [pltpu.make_async_copy(via, dst, out_sems.at[i]) for i, (_, via, dst) in enumerate(pieces[1:])]
    outs += [
        pltpu.make_async_copy(via, dst, out_sems.at[len(outs) + i])
        for i, (via, dst) in enumerate([(dfg, dfg_out), (ufg, ufg_out)])
    ]
    for copy in ins:
        copy.start()
    ins[0].wait()
    for j in range(NZ - 1):
        dfg[:, j * 128 : (j + 1) * 128] = adapter_scale * sums[j].astype(F32)
    ufg[...] = adapter_scale * sums[NZ - 1].astype(F32)
    outs[-2].start()
    outs[-1].start()
    for before, after in zip(ins[1:], outs):
        before.wait()
        after.start()
    for copy in outs:
        copy.wait()


def per_device(
    normed_layer_input,
    queries,
    saved_key_rows,
    saved_value_rows,
    attention_output_gradient,
    finisher_token_mask,
    response_length,
    value_weight_matrix,
    adapter_down_factor,
    adapter_up_factor,
):
    hbm = pl.BlockSpec(memory_space=pltpu.HBM)
    dma = pltpu.SemaphoreType.DMA
    outs = pl.pallas_call(
        kernel,
        out_shape=(
            jax.ShapeDtypeStruct((CTX, FEATS), BF16),
            jax.ShapeDtypeStruct((RESP, FEATS), BF16),
            jax.ShapeDtypeStruct((CTX, HD), BF16),
            jax.ShapeDtypeStruct((NZ, RANK, HD), BF16),
        ),
        in_specs=[hbm] * 10,
        out_specs=(hbm,) * 4,
        scratch_shapes=[
            pltpu.VMEM((CTX, FEATS), BF16),
            pltpu.VMEM((RESP, FEATS), BF16),
            pltpu.VMEM((CTX, HD), BF16),
            pltpu.VMEM((CTX, HD), BF16),
            pltpu.VMEM((RESP, FEATS), BF16),
            pltpu.VMEM((RANK, FEATS), BF16),
            pltpu.VMEM((1, RESP), jnp.int32),
            pltpu.SMEM((1,), jnp.int32),
            pltpu.VMEM((RANK, HD), BF16),
            pltpu.VMEM((NY, NZ, ROWS, FEATS), BF16),
            pltpu.VMEM((NY, CTX, HD), BF16),
            pltpu.VMEM((SEEN[0], FEATS), F32),
            pltpu.VMEM((SEEN[1], FEATS), F32),
            pltpu.VMEM((SEEN[0], FEATS), BF16),
            pltpu.VMEM((SEEN[1], FEATS), BF16),
            pltpu.VMEM((NY, 4, ROWS, HD), BF16),
            pltpu.VMEM((NY, 4, ROWS, HD), BF16),
            pltpu.VMEM((NY, 2, ROWS, HD), BF16),
            pltpu.VMEM((NZ, RANK, HD), BF16),
            pltpu.VMEM((NZ, RANK, HD), BF16),
            pltpu.VMEM((NX * NC, RANK, HD), BF16),
            pltpu.VMEM((RANK, HD), BF16),
            pltpu.VMEM((CTX, FEATS), BF16),
            pltpu.VMEM((RESP, FEATS), BF16),
            pltpu.VMEM((CTX, HD), BF16),
            dma((10,)),
            dma((5,)),
            dma((NY - 1,)),
            dma,
            dma((2, NZ - 1)),
            dma((2, NZ - 1)),
            dma((2, NX - 1)),
            dma((2, NX - 1)),
            dma((2, NX)),
            dma((2, NX)),
            dma((NY - 1,)),
            dma((NY - 1,)),
            dma((NY - 1,)),
            dma((NY - 1,)),
            dma((NY - 1,)),
            dma((NY - 1,)),
            dma((NZ - 1,)),
            dma((NZ - 1,)),
            dma((NX * NC - 1,)),
            dma((NX * NC - 1,)),
            dma((NZ - 1,)),
            dma((NZ - 1,)),
        ],
        compiler_params=pltpu.CompilerParams(
            collective_id=0, has_side_effects=True, vmem_limit_bytes=VMEM_LIMIT
        ),
    )(
        normed_layer_input,
        queries,
        saved_key_rows,
        saved_value_rows,
        attention_output_gradient,
        finisher_token_mask.reshape(1, RESP),
        response_length,
        value_weight_matrix,
        adapter_down_factor.T,
        adapter_up_factor,
    )
    lig, qg, kg, dfg_t, ufg = pl.pallas_call(
        hand_on,
        out_shape=(
            jax.ShapeDtypeStruct((CTX, FEATS), BF16),
            jax.ShapeDtypeStruct((RESP, FEATS), BF16),
            jax.ShapeDtypeStruct((CTX, HD), BF16),
            jax.ShapeDtypeStruct((RANK, FEATS), F32),
            jax.ShapeDtypeStruct((RANK, HD), F32),
        ),
        in_specs=[hbm] * 4,
        out_specs=(hbm,) * 5,
        scratch_shapes=[
            pltpu.VMEM((CTX, FEATS), BF16),
            pltpu.VMEM((RESP, FEATS), BF16),
            pltpu.VMEM((CTX, HD), BF16),
            pltpu.VMEM((NZ, RANK, HD), BF16),
            pltpu.VMEM((RANK, FEATS), F32),
            pltpu.VMEM((RANK, HD), F32),
            dma((9,)),
            dma((10,)),
        ],
        compiler_params=pltpu.CompilerParams(vmem_limit_bytes=VMEM_LIMIT),
    )(*outs)
    return (lig, qg, kg, dfg_t.T, ufg)


def solution(mesh):
    in_specs = (
        P("dp", "tp"),
        P("dp", "tp"),
        P("dp", "tp"),
        P("dp", "tp"),
        P("dp", "tp"),
        P("dp"),
        P("dp"),
        P("tp", None),
        P("tp", None),
        P(None, "tp"),
    )
    out_specs = (P("dp", "tp"), P("dp", "tp"), P("dp", "tp"), P("tp", None), P(None, "tp"))
    return jax.shard_map(
        per_device, mesh=mesh, in_specs=in_specs, out_specs=out_specs, check_vma=False
    )
```
